256 devices in a mesh: ctx: 32 (over z_lo, y, core), head: 8 (over z_hi, x).
Axes of the slice: x: 4, y: 4, z: 8 (z_hi: 2, z_lo: 4; z = z_hi * 4 + z_lo), core: 2. Of those that a mesh axis runs over, the one named last changes fastest.
Arguments:
- hidden_states: bfloat16 [4096, 7168], P('ctx', 'head'), may hold values from -384 to 384
- down_query: bfloat16 [7168, 1536], P('head'), may hold values from -0.0625 to 0.0625
- down_latent: bfloat16 [7168, 576], P('head'), may hold values from -0.0625 to 0.0625
- query_gain: float32 [1536], replicated, may hold values from 0.1 to 1.9
- latent_gain: float32 [512], replicated, may hold values from 0.1 to 1.9
- up_query: bfloat16 [1536, 12288], P(None, 'head'), may hold values from -0.15625 to 0.15625
- up_key: bfloat16 [512, 8192], P(None, 'head'), may hold values from -0.375 to 0.375
- up_value: bfloat16 [512, 8192], P(None, 'head'), may hold values from -0.75 to 0.75
- owner_table: int32 [64], replicated, may hold values from 0 to 63, each once
Outputs:
- attended: bfloat16 [4096, 8192], P('ctx', 'head')
The draws below stay inside these ranges and needn't reach their ends.
Inputs may be any that keep to these rules, and one draw needn't show every extreme that they name: Block b of the sequence, positions 64 * b to 64 * b + 63, lies in token rows 64 * owner_table[b] to 64 * owner_table[b] + 63; each row block holds exactly one sequence block.
All inputs are finite; a program needn't handle non-finite values.
Results may differ from the reference program's by a relative error of at most 0.035.
Values may be sent and summed in bfloat16 or wider, within the bound.
No kernel may reach another device: no remote copies, remote signals or barrier semaphores. Data moves between devices by JAX's collectives and lax.ppermute only.
A program may use at most 128 MiB of HBM per device.

```python
import math
import jax
import jax.numpy as jnp
from jax import lax

D = 7168
QL = 1536
KVL = 512
RD = 64
NOPE = 128
VD = 128
HEADS = 64
TOKENS = 4096
BLK = 64
NBLK = 64


def draw_hidden_states(key, part):
    key = jax.random.fold_in(key, 11)
    base_key = jax.random.fold_in(key, 0)
    result = jnp.clip(jax.random.normal(base_key, (TOKENS, D), jnp.float32), -4.0, 4.0)
    return result.astype(jnp.bfloat16)


def shard_levels(key, extent, cuts, low, top_value):
    def one(position, blocks):
        heights = jax.random.uniform(jax.random.fold_in(jax.random.fold_in(key, 6), position), (blocks,), jnp.float32, low / len(cuts), top_value / len(cuts))
        return jnp.repeat(jnp.exp(heights), extent[position] // blocks).reshape((-1,) + (1,) * (len(extent) - position - 1))

    level = one(*cuts[0])
    for cut in cuts[1:]:
        level = level * one(*cut)
    return level


def normal_values(key, shape, deviation, most, cuts=(), kind=jnp.bfloat16):
    factor_of = shard_levels(key, shape, cuts, -0.22, 0.18) if cuts else 1.0
    entries = jax.random.normal(key, shape, jnp.float32) * deviation * factor_of
    return jnp.minimum(jnp.maximum(entries, -most), most).astype(kind)


def setup_inputs(seed: int = 0) -> dict:
    key_list = jax.random.split(jax.random.key(seed), 10)
    return {
        "hidden_states": draw_hidden_states(jax.random.fold_in(key_list[9], 71), 0),
        "down_query": normal_values(key_list[1], (D, QL), D ** -0.5, 0.0625, ((0, 8),)),
        "down_latent": normal_values(key_list[2], (D, KVL + RD), D ** -0.5, 0.0625, ((0, 8),)),
        "query_gain": jnp.clip(1.0 + 0.18 * jax.random.normal(key_list[3], (QL,), jnp.float32), 0.1, 1.9),
        "latent_gain": jnp.clip(1.0 + 0.18 * jax.random.normal(key_list[4], (KVL,), jnp.float32), 0.1, 1.9),
        "up_query": normal_values(key_list[5], (QL, HEADS * (NOPE + RD)), QL ** -0.5, 0.15625, ((1, 8),)),
        "up_key": normal_values(key_list[6], (KVL, HEADS * NOPE), 256 ** -0.5, 0.375, ((1, 8),)),
        "up_value": normal_values(key_list[7], (KVL, HEADS * VD), 64 ** -0.5, 0.75, ((1, 8),)),
        "owner_table": jax.random.permutation(key_list[8], NBLK).astype(jnp.int32),
    }


def rope_rotate(values, positions):
    half_width = values.shape[-1] // 2
    step_index = jnp.arange(half_width).astype(jnp.float32)
    frequency = jnp.exp(step_index * (-math.log(10000.0) / half_width))
    angle_table = positions.astype(jnp.float32)[..., None] * frequency
    cosines = jnp.cos(angle_table)
    sine_table = jnp.sin(angle_table)
    first_half = values[..., :half_width]
    second_half = values[..., half_width:]
    return jnp.concatenate([first_half * cosines - second_half * sine_table, second_half * cosines + first_half * sine_table], axis=-1)

def rms_scale(vector, scales):
    return vector * lax.rsqrt(lax.optimization_barrier(jnp.mean(vector * vector, axis=-1, keepdims=True)) + 1e-06) * scales

def block_positions(owner_table, row_index, block_rows):
    slot_index = row_index // block_rows
    block_count = owner_table.shape[0]
    match_table = (owner_table[None, :] == slot_index[:, None]).astype(jnp.int32)
    block_index = lax.optimization_barrier(jnp.sum(match_table * jnp.arange(block_count, dtype=jnp.int32)[None, :], axis=1))
    return (block_index * block_rows + row_index % block_rows).astype(jnp.int32)

def reference(hidden_states, down_query, down_latent, query_gain, latent_gain, up_query, up_key, up_value, owner_table):
    row_index = jnp.arange(TOKENS, dtype=jnp.int32)
    positions = block_positions(owner_table, row_index, BLK)
    query_down = jnp.dot(hidden_states, down_query, preferred_element_type=jnp.float32)
    latent_down = jnp.dot(hidden_states, down_latent, preferred_element_type=jnp.float32)
    query_latent = rms_scale(query_down, query_gain).astype(jnp.bfloat16)
    key_latent = rms_scale(latent_down[:, :KVL], latent_gain).astype(jnp.bfloat16)
    key_rope = rope_rotate(latent_down[:, KVL:], positions).astype(jnp.bfloat16)
    key_block = jnp.concatenate([key_latent, key_rope], axis=1)
    query_full = jnp.dot(query_latent, up_query, preferred_element_type=jnp.float32).reshape(TOKENS, HEADS, NOPE + RD)
    query_nope = query_full[:, :, :NOPE].astype(jnp.bfloat16)
    query_rope = rope_rotate(query_full[:, :, NOPE:], positions[:, None]).astype(jnp.bfloat16)
    nope_heads = jnp.transpose(query_nope, (1, 0, 2))
    rope_heads = jnp.transpose(query_rope, (1, 0, 2))
    key_heads = jnp.transpose(up_key.reshape(KVL, HEADS, NOPE), (1, 0, 2))
    value_heads = jnp.transpose(up_value.reshape(KVL, HEADS, VD), (1, 0, 2))
    causal = positions[None, :] <= positions[:, None]
    score_scale = 1.0 / math.sqrt(NOPE + RD)

    def per_head(operands):
        nope_part, rope_part, key_up, value_up = operands
        absorbed = jnp.dot(nope_part, key_up.T, preferred_element_type=jnp.float32).astype(jnp.bfloat16)
        queries = jnp.concatenate([absorbed, rope_part], axis=1)
        scores = jnp.dot(queries, key_block.T, preferred_element_type=jnp.float32) * score_scale
        scores = jnp.where(causal, scores, -jnp.inf)
        row_top = lax.optimization_barrier(jnp.max(scores, axis=1, keepdims=True))
        exp_terms = jnp.exp(scores - row_top)
        denominator = lax.optimization_barrier(jnp.sum(exp_terms, axis=1, keepdims=True))
        probabilities = exp_terms.astype(jnp.bfloat16)
        latent_mix = (jnp.dot(probabilities, key_latent, preferred_element_type=jnp.float32) / denominator).astype(jnp.bfloat16)
        return jnp.dot(latent_mix, value_up, preferred_element_type=jnp.float32).astype(jnp.bfloat16)
    outputs = lax.map(per_head, (nope_heads, rope_heads, key_heads, value_heads))
    return jnp.transpose(outputs, (1, 0, 2)).reshape(TOKENS, HEADS * VD)
```

```python
import functools
import math

import jax
import jax.numpy as jnp
from jax import lax
from jax.experimental import pallas as pl
from jax.experimental.pallas import tpu as pltpu
from jax.sharding import PartitionSpec as P

RD = 64
NOPE = 128
VD = 128
KVL = 512
BLK = 64
LANES = 128
WIDE = KVL + LANES
CHUNK = 32
PACK = CHUNK * (KVL + RD) // LANES
TILE = 512
SPAN = 256
NEG = -1e30
SCALE = 1.0 / math.sqrt(NOPE + RD)
LOG2E = math.log2(math.e)
NX, NY, NZ, NZL, NC = 4, 4, 8, 4, 2
AXES = ("ctx", "head")
OFFSETS = (0, -1, 1, 2)
CONTRACT_LAST = (((1,), (1,)), ((), ()))
VMEM = pl.BlockSpec(memory_space=pltpu.VMEM)
SMEM = pl.BlockSpec(memory_space=pltpu.SMEM)


def angles(positions):
    half_width = RD // 2
    step_index = jnp.arange(half_width).astype(jnp.float32)
    frequency = jnp.exp(step_index * (-math.log(10000.0) / half_width))
    return positions.astype(jnp.float32)[..., None] * frequency


def rotary_tables(positions):
    table = angles(positions)
    cosines, sines = jnp.cos(table), jnp.sin(table)
    return (
        jnp.concatenate([cosines, cosines], axis=-1),
        jnp.concatenate([-sines, sines], axis=-1),
    )


def block_positions(owner_table, row_index, block_rows):
    slot_index = row_index // block_rows
    block_count = owner_table.shape[0]
    match_table = (owner_table[None, :] == slot_index[:, None]).astype(jnp.int32)
    block_index = jnp.sum(match_table * jnp.arange(block_count, dtype=jnp.int32)[None, :], axis=1)
    return block_index * block_rows + row_index % block_rows


def flat(x, y, z, c):
    ctx = ((z % NZL) * NY + y) * NC + c
    return ctx * (2 * NX) + (z // NZL) * NX + x


def send(value, move):
    pairs = []
    for x in range(NX):
        for y in range(NY):
            for z in range(NZ):
                for c in range(NC):
                    tx, ty, tz, tc = move(x, y, z, c)
                    pairs.append((flat(x, y, z, c), flat(tx % NX, ty % NY, tz % NZ, tc)))
    return lax.ppermute(value, AXES, pairs)


def along_x(step):
    return lambda x, y, z, c: (x + step, y, z, c)


def step_z(z, step):
    return z + step if step != 2 or z % 2 == 0 else z - step


def along_first(step):
    return lambda x, y, z, c: (x, y + step, z, c) if c == 0 else (x, y, step_z(z, step), c)


def along_second(step):
    return lambda x, y, z, c: (x, y, step_z(z, step), c) if c == 0 else (x, y + step, z, c)


def other_half(x, y, z, c):
    return (x, y, z + NZL, c)


def other_core(x, y, z, c):
    return (x, y, z, 1 - c)


def gather_ring(value, along):
    return [value] + [send(value, along(-offset)) for offset in OFFSETS[1:]]


def kernel_call(kernel, out_shape, in_specs, scratch, flops, moved, limit=32):
    return pl.pallas_call(
        kernel,
        out_shape=out_shape,
        in_specs=in_specs,
        out_specs=jax.tree.map(lambda _: VMEM, out_shape),
        scratch_shapes=scratch,
        compiler_params=pltpu.CompilerParams(vmem_limit_bytes=limit * 2**20),
        cost_estimate=pl.CostEstimate(flops=flops, bytes_accessed=moved, transcendentals=0),
    )


def down_kernel(packed, x_ref, hidden, weight, *refs):
    pieces, part = refs[:NX], refs[NX]
    part[...] = jnp.dot(hidden[...], weight[...], preferred_element_type=jnp.float32)
    for step, piece in enumerate(pieces):
        start = pl.multiple_of(((x_ref[0] + step) & (NX - 1)) * CHUNK, CHUNK)
        rows = part[pl.ds(start, CHUNK), :]
        if packed:
            for tile in range(KVL // LANES):
                piece[tile * CHUNK : (tile + 1) * CHUNK] = rows[:, tile * LANES : (tile + 1) * LANES]
            rope = rows[:, KVL:]
            piece[KVL // LANES * CHUNK :] = jnp.concatenate(
                [rope[: CHUNK // 2], rope[CHUNK // 2 :]], axis=1
            )
        else:
            piece[...] = rows


def down(packed, x_index, hidden, weight):
    rows, depth = hidden.shape
    columns = weight.shape[1]
    shape = (PACK, LANES) if packed else (CHUNK, columns)
    return kernel_call(
        functools.partial(down_kernel, packed),
        [jax.ShapeDtypeStruct(shape, jnp.float32)] * NX,
        [SMEM, VMEM, VMEM],
        [pltpu.VMEM((rows, columns), jnp.float32)],
        2 * rows * depth * columns,
        2 * depth * columns,
    )(x_index, hidden, weight)


def reduce_x(pieces):
    own, one, two, three = pieces
    return own + send(one, along_x(1)) + send(two, along_x(2)) + send(three, along_x(3))


def exchange_halves(values, lanes):
    half = RD // 2
    left = pltpu.roll(values, LANES - half, 1)
    right = pltpu.roll(values, half, 1)
    return jnp.where((lanes & half) == 0, left, right)


def key_norm_kernel(own, other, gain, cosines, sines, out):
    total = own[...] + other[...]
    tiles = [total[tile * CHUNK : (tile + 1) * CHUNK] for tile in range(KVL // LANES)]
    squares = sum(tile * tile for tile in tiles)
    factor = lax.rsqrt(jnp.sum(squares, axis=1, keepdims=True) * (1.0 / KVL) + 1e-06)
    for index, tile in enumerate(tiles):
        out[index * CHUNK : (index + 1) * CHUNK] = (
            tile * factor * gain[index : index + 1, :]
        ).astype(out.dtype)
    rope = total[KVL // LANES * CHUNK :]
    lanes = lax.broadcasted_iota(jnp.int32, rope.shape, 1)
    out[KVL // LANES * CHUNK :] = (
        rope * cosines[...] + exchange_halves(rope, lanes) * sines[...]
    ).astype(out.dtype)


def query_norm_kernel(own, other, gain, out):
    total = own[...] + other[...]
    mean = jnp.sum(total * total, axis=1, keepdims=True) * (1.0 / total.shape[1])
    out[...] = (total * lax.rsqrt(mean + 1e-06) * gain[...]).astype(out.dtype)


def query_kernel(x_ref, piece0, piece1, piece2, piece3, up_query, up_key, cosines, sines, out, rows):
    for step, piece in enumerate((piece0, piece1, piece2, piece3)):
        start = pl.multiple_of(((x_ref[0] + step) & (NX - 1)) * CHUNK, CHUNK)
        rows[pl.ds(start, CHUNK), :] = piece[...]
    tokens = rows.shape[0]
    lanes = lax.broadcasted_iota(jnp.int32, (tokens, LANES), 1)
    pair = 2 * (NOPE + RD)
    for index in range(up_query.shape[1] // pair):
        full = jnp.dot(
            rows[...],
            up_query[:, index * pair : (index + 1) * pair],
            preferred_element_type=jnp.float32,
        )
        first, second, third = (full[:, i * LANES : (i + 1) * LANES] for i in range(3))
        second_half, third_half = pltpu.roll(second, RD, 1), pltpu.roll(third, RD, 1)
        heads = (
            (first, second),
            (jnp.where(lanes < RD, second_half, third_half), third_half),
        )
        for offset, (nope, rope) in enumerate(heads):
            head = 2 * index + offset
            absorbed = lax.dot_general(
                nope.astype(jnp.bfloat16),
                up_key[:, head * NOPE : (head + 1) * NOPE],
                CONTRACT_LAST,
                preferred_element_type=jnp.float32,
            )
            out[head * tokens : (head + 1) * tokens, :KVL] = absorbed.astype(out.dtype)
            turned = rope * cosines[...] + exchange_halves(rope, lanes) * sines[...]
            out[head * tokens : (head + 1) * tokens, KVL:] = jnp.where(
                lanes < RD, turned, 0.0
            ).astype(out.dtype)


def attend_kernel(parts, first, last, *refs):
    refs = list(refs)
    queries, key_at, query_at = refs[:3]
    sources, refs = refs[3 : 3 + parts], refs[3 + parts :]
    if not first:
        (old_top, old_total, old_acc), refs = refs[:3], refs[3:]
    if last:
        up_value, out, refs = refs[0], refs[1], refs[2:]
    else:
        (new_top, new_total, new_acc), refs = refs[:3], refs[3:]
    keys, scores, acc = refs

    chunks = TILE // CHUNK
    for part, source in enumerate(sources):
        for chunk in range(chunks):
            to, at = part * TILE + chunk * CHUNK, chunk * PACK
            for tile in range(KVL // LANES):
                keys[to : to + CHUNK, tile * LANES : (tile + 1) * LANES] = source[
                    at + tile * CHUNK : at + (tile + 1) * CHUNK
                ]
            rope = source[at + KVL // LANES * CHUNK : at + PACK]
            keys[to : to + CHUNK // 2, KVL:] = rope
            keys[to + CHUNK // 2 : to + CHUNK, KVL:] = jnp.concatenate(
                [rope[:, RD:], rope[:, :RD]], axis=1
            )

    tokens = query_at.shape[0]
    rows_at = jnp.concatenate([query_at[...]] * (SPAN // tokens), axis=0)
    spans = queries.shape[0] // SPAN
    tops, totals, weights = {}, {}, {}

    def score(span, tile):
        view = slice(tile * TILE, (tile + 1) * TILE)
        value = lax.dot_general(
            queries[span * SPAN : (span + 1) * SPAN],
            keys[view],
            CONTRACT_LAST,
            preferred_element_type=jnp.float32,
        )
        value = jnp.where(key_at[:, view] <= rows_at, value, NEG)
        scores[span % 2, :, view] = value
        for lane in range(TILE // LANES):
            column = value[:, lane * LANES : (lane + 1) * LANES]
            tops[span] = jnp.maximum(tops[span], column) if span in tops else column

    def mix(span, tile):
        rows = slice(span * SPAN, (span + 1) * SPAN)
        view = slice(tile * TILE, (tile + 1) * TILE)
        if tile == 0:
            top = jnp.max(tops[span], axis=1, keepdims=True)
            if not first:
                before = old_top[rows, :1]
                top = jnp.maximum(top, before)
                weights[span] = jnp.exp2((before - top) * (SCALE * LOG2E))
            tops[span] = top
        terms = jnp.exp2((scores[span % 2, :, view] - tops[span]) * (SCALE * LOG2E))
        for lane in range(TILE // LANES):
            column = terms[:, lane * LANES : (lane + 1) * LANES]
            totals[span] = totals[span] + column if span in totals else column
        value = jnp.dot(
            terms.astype(jnp.bfloat16), keys[view, :KVL], preferred_element_type=jnp.float32
        )
        if tile > 0:
            value = acc[span % 2] + value
        elif not first:
            value = old_acc[rows] * weights[span] + value
        if tile < parts - 1:
            acc[span % 2] = value
            return
        total = jnp.sum(totals[span], axis=1, keepdims=True)
        if not first:
            total = total + old_total[rows, :1] * weights[span]
        if not last:
            new_acc[rows] = value
            new_top[rows] = jnp.broadcast_to(tops[span], (SPAN, LANES))
            new_total[rows] = jnp.broadcast_to(total, (SPAN, LANES))
            return
        latent_mix = (value / total).astype(jnp.bfloat16)
        for index in range(SPAN // tokens):
            head = span * (SPAN // tokens) + index
            columns = slice(head * VD, (head + 1) * VD)
            out[:, columns] = jnp.dot(
                latent_mix[index * tokens : (index + 1) * tokens],
                up_value[:, columns],
                preferred_element_type=jnp.float32,
            ).astype(out.dtype)

    for span in range(spans + 1):
        for tile in range(parts):
            if span < spans:
                score(span, tile)
            if span > 0:
                mix(span - 1, tile)


def attend(queries, key_at, query_at, sources, state=(), up_value=None):
    rows, parts = queries.shape[0], len(sources)
    tokens = query_at.shape[0]
    if up_value is not None:
        out_shape = jax.ShapeDtypeStruct((tokens, rows // tokens * VD), jnp.bfloat16)
    else:
        out_shape = [
            jax.ShapeDtypeStruct((rows, LANES), jnp.float32),
            jax.ShapeDtypeStruct((rows, LANES), jnp.float32),
            jax.ShapeDtypeStruct((rows, KVL), jnp.float32),
        ]
    operands = [queries, key_at, query_at, *sources, *state]
    if up_value is not None:
        operands.append(up_value)
    keys = parts * TILE
    return kernel_call(
        functools.partial(attend_kernel, parts, not state, up_value is not None),
        out_shape,
        [VMEM] * len(operands),
        [
            pltpu.VMEM((keys, WIDE), jnp.bfloat16),
            pltpu.VMEM((2, SPAN, keys), jnp.float32),
            pltpu.VMEM((2, SPAN, KVL), jnp.float32),
        ],
        2 * rows * keys * (KVL + WIDE),
        keys * WIDE * 4,
    )(*operands)


def chunk_rows(x, y, zl, core):
    ring = jnp.array(OFFSETS, jnp.int32)
    first, second, third = ring[None, :, None], ring[:, None, None], ring[None, None, :]
    y_at = (y + jnp.where(core == 0, first, second)) % NY
    z_at = (zl + jnp.where(core == 0, second, first)) % NZL
    x_at = (x + third) % NX
    return (((z_at * NY + y_at) * NC + core) * (NX * CHUNK) + x_at * CHUNK).reshape(-1)


def body(
    hidden_states,
    down_query,
    down_latent,
    query_gain,
    latent_gain,
    up_query,
    up_key,
    up_value,
    owner_table,
):
    tok_rows = hidden_states.shape[0]
    local_heads = up_key.shape[1] // NOPE
    ctx = lax.axis_index("ctx")
    head = lax.axis_index("head")
    x = head % NX
    c, y, zl = ctx % NC, (ctx // NC) % NY, ctx // (NC * NY)
    x_index = x.reshape(1)

    firsts = jnp.concatenate([chunk_rows(x, y, zl, c), chunk_rows(x, y, zl, 1 - c)])
    starts = block_positions(owner_table, firsts, BLK)
    key_at = (starts[:, None] + jnp.arange(CHUNK, dtype=jnp.int32)[None, :]).reshape(1, -1)
    own_rows = ctx * tok_rows + jnp.arange(tok_rows, dtype=jnp.int32)
    own_positions = block_positions(owner_table, own_rows, BLK)
    key_cos, key_sin = (
        jnp.concatenate([table[: CHUNK // 2], table[CHUNK // 2 :]], axis=1)
        for table in rotary_tables(starts[0] + jnp.arange(CHUNK, dtype=jnp.int32))
    )
    query_cos, query_sin = (
        jnp.concatenate([table, table], axis=1) for table in rotary_tables(own_positions)
    )

    key_half = reduce_x(down(True, x_index, hidden_states, down_latent))
    query_half = reduce_x(down(False, x_index, hidden_states, down_query))
    key_pack = kernel_call(
        key_norm_kernel,
        jax.ShapeDtypeStruct((PACK, LANES), jnp.bfloat16),
        [VMEM] * 5,
        [],
        10 * PACK * LANES,
        10 * PACK * LANES,
    )(key_half, send(key_half, other_half), latent_gain.reshape(-1, LANES), key_cos, key_sin)
    key_own = jnp.concatenate(gather_ring(key_pack, along_x), axis=0)
    key_first = jnp.concatenate(gather_ring(key_own, along_first), axis=0)
    near = gather_ring(key_first, along_second)
    far = [send(part, other_core) for part in near]

    query_latent = kernel_call(
        query_norm_kernel,
        jax.ShapeDtypeStruct(query_half.shape, jnp.bfloat16),
        [VMEM] * 3,
        [],
        10 * query_half.size,
        10 * query_half.size,
    )(query_half, send(query_half, other_half), query_gain.reshape(1, -1))
    pieces = [query_latent] + [send(query_latent, along_x(-step)) for step in (1, 2, 3)]
    queries = kernel_call(
        query_kernel,
        jax.ShapeDtypeStruct((local_heads * tok_rows, WIDE), jnp.bfloat16),
        [SMEM] + [VMEM] * 8,
        [pltpu.VMEM((tok_rows, up_query.shape[0]), jnp.bfloat16)],
        2 * tok_rows * (up_query.size + up_key.size),
        2 * (up_query.size + up_key.size),
    )(x_index, *pieces, up_query, up_key, query_cos, query_sin)

    query_at = own_positions.reshape(-1, 1)
    half = key_at.shape[1] // 2
    state = attend(queries, key_at[:, :half], query_at, near)
    return attend(queries, key_at[:, half:], query_at, far, state, up_value)


def solution(mesh):
    placed = (
        P("ctx", "head"),
        P("head", None),
        P("head", None),
        P(),
        P(),
        P(None, "head"),
        P(None, "head"),
        P(None, "head"),
        P(),
    )
    return jax.shard_map(
        body, mesh=mesh, in_specs=placed, out_specs=P("ctx", "head"), check_vma=False
    )
```

```python
import functools
import math

import jax
import jax.numpy as jnp
from jax import lax
from jax.experimental import pallas as pl
from jax.experimental.pallas import tpu as pltpu
from jax.sharding import PartitionSpec as P

RD = 64
NOPE = 128
VD = 128
KVL = 512
BLK = 64
LANES = 128
WIDE = KVL + LANES
CHUNK = 32
PACK = CHUNK * (KVL + RD) // LANES
QPACK = 12
TILE = 512
SPAN = 256
NEG = -1e30
SCALE = 1.0 / math.sqrt(NOPE + RD)
LOG2E = math.log2(math.e)
NX, NY, NZ, NZL, NC = 4, 4, 8, 4, 2
AXES = ("ctx", "head")
OFFSETS = (0, -1, 1, 2)
CONTRACT_LAST = (((1,), (1,)), ((), ()))
VMEM = pl.BlockSpec(memory_space=pltpu.VMEM)
SMEM = pl.BlockSpec(memory_space=pltpu.SMEM)
FAR = pl.BlockSpec(memory_space=pltpu.HBM)


def angles(positions):
    half_width = RD // 2
    step_index = jnp.arange(half_width).astype(jnp.float32)
    frequency = jnp.exp(step_index * (-math.log(10000.0) / half_width))
    return positions.astype(jnp.float32)[..., None] * frequency


def rotary_tables(positions):
    table = angles(positions)
    cosines, sines = jnp.cos(table), jnp.sin(table)
    return (
        jnp.concatenate([cosines, cosines], axis=-1),
        jnp.concatenate([-sines, sines], axis=-1),
    )


def block_positions(owner_table, row_index, block_rows):
    slot_index = row_index // block_rows
    block_count = owner_table.shape[0]
    match_table = (owner_table[None, :] == slot_index[:, None]).astype(jnp.int32)
    block_index = jnp.sum(match_table * jnp.arange(block_count, dtype=jnp.int32)[None, :], axis=1)
    return block_index * block_rows + row_index % block_rows


def flat(x, y, z, c):
    ctx = ((z % NZL) * NY + y) * NC + c
    return ctx * (2 * NX) + (z // NZL) * NX + x


def send(value, move):
    pairs = []
    for x in range(NX):
        for y in range(NY):
            for z in range(NZ):
                for c in range(NC):
                    tx, ty, tz, tc = move(x, y, z, c)
                    pairs.append((flat(x, y, z, c), flat(tx % NX, ty % NY, tz % NZ, tc)))
    return lax.ppermute(value, AXES, pairs)


def along_x(step):
    return lambda x, y, z, c: (x + step, y, z, c)


def step_z(z, step):
    return z - step if abs(step) == 2 and z % 2 else z + step


def along_first(step):
    return lambda x, y, z, c: (x, y + step, z, c) if c == 0 else (x, y, step_z(z, step), c)


def along_second(step):
    return lambda x, y, z, c: (x, y, step_z(z, step), c) if c == 0 else (x, y + step, z, c)


def other_half(x, y, z, c):
    return (x, y, z + NZL, c)


def other_core(x, y, z, c):
    return (x, y, z, 1 - c)


def gather_ring(value, along):
    return [value] + [send(value, along(-offset)) for offset in OFFSETS[1:]]


def kernel_call(kernel, out_shape, in_specs, scratch, flops, moved, limit=32):
    return pl.pallas_call(
        kernel,
        out_shape=out_shape,
        in_specs=in_specs,
        out_specs=jax.tree.map(lambda _: VMEM, out_shape),
        scratch_shapes=scratch,
        compiler_params=pltpu.CompilerParams(vmem_limit_bytes=limit * 2**20),
        cost_estimate=pl.CostEstimate(flops=flops, bytes_accessed=moved, transcendentals=0),
    )


def down_kernel(x_ref, hidden_far, latent_far, query_far, *refs):
    pieces, (hidden, latent, query, part, sems) = refs[:NX], refs[NX:]
    half = latent.shape[0] // 2
    span = query.shape[1] // 3
    loads = [pltpu.make_async_copy(hidden_far, hidden, sems.at[0])]
    for index in range(2):
        rows = pl.ds(index * half, half)
        loads.append(
            pltpu.make_async_copy(latent_far.at[rows], latent.at[rows], sems.at[1 + index])
        )
    for index in range(3):
        columns = pl.ds(index * span, span)
        loads.append(
            pltpu.make_async_copy(
                query_far.at[:, columns], query.at[:, columns], sems.at[3 + index]
            )
        )
    for load in loads:
        load.start()
    for load in loads[:3]:
        load.wait()
    wide = latent.shape[0]
    part[:, :wide] = lax.dot_general(
        hidden[...], latent[...], CONTRACT_LAST, preferred_element_type=jnp.float32
    )
    starts = [pl.multiple_of(((x_ref[0] + step) & (NX - 1)) * CHUNK, CHUNK) for step in range(NX)]
    for start, piece in zip(starts, pieces):
        rows = part[pl.ds(start, CHUNK), :wide]
        for tile in range(KVL // LANES):
            piece[tile * CHUNK : (tile + 1) * CHUNK] = rows[:, tile * LANES : (tile + 1) * LANES]
        rope = rows[:, KVL:]
        piece[KVL // LANES * CHUNK : PACK] = jnp.concatenate(
            [rope[: CHUNK // 2], rope[CHUNK // 2 :]], axis=1
        )
    for index in range(3):
        loads[3 + index].wait()
        part[:, :span] = jnp.dot(
            hidden[...],
            query[:, index * span : (index + 1) * span],
            preferred_element_type=jnp.float32,
        )
        for start, piece in zip(starts, pieces):
            for tile in range(span // LANES):
                to = PACK + (index * (span // LANES) + tile) * CHUNK
                piece[to : to + CHUNK] = part[
                    pl.ds(start, CHUNK), tile * LANES : (tile + 1) * LANES
                ]


def down(x_index, hidden, latent, query):
    rows, depth = hidden.shape
    shape = (PACK + QPACK * CHUNK, LANES)
    return kernel_call(
        down_kernel,
        [jax.ShapeDtypeStruct(shape, jnp.float32)] * NX,
        [SMEM, FAR, FAR, FAR],
        [
            pltpu.VMEM(hidden.shape, hidden.dtype),
            pltpu.VMEM(latent.shape, latent.dtype),
            pltpu.VMEM(query.shape, query.dtype),
            pltpu.VMEM((rows, 5 * LANES), jnp.float32),
            pltpu.SemaphoreType.DMA((6,)),
        ],
        2 * rows * (latent.size + query.size),
        2 * (latent.size + query.size),
        limit=63,
    )(x_index, hidden, latent, query)


def sum_kernel(own, one, two, three, out):
    out[...] = own[...] + one[...] + two[...] + three[...]


def join_kernel(rows, *refs):
    pieces, out = refs[:-1], refs[-1]
    for index, piece in enumerate(pieces):
        out[index * rows : (index + 1) * rows] = piece[:rows]


def join(pieces, rows):
    shape = (len(pieces) * rows, LANES)
    size = len(pieces) * rows * LANES
    return kernel_call(
        functools.partial(join_kernel, rows),
        jax.ShapeDtypeStruct(shape, pieces[0].dtype),
        [VMEM] * len(pieces),
        [],
        size,
        4 * size,
    )(*pieces)


def load_kernel(count, *refs):
    sources, outs, sems = refs[:count], refs[count : 2 * count], refs[2 * count]
    loads = []
    for source, out in zip(sources, outs):
        rows = source.shape[0] // 2
        for half in range(2):
            view = pl.ds(half * rows, rows)
            loads.append(
                pltpu.make_async_copy(source.at[view], out.at[view], sems.at[len(loads)])
            )
    for load in loads:
        load.start()
    for load in loads:
        load.wait()


def load_weights(*weights):
    return kernel_call(
        functools.partial(load_kernel, len(weights)),
        [jax.ShapeDtypeStruct(weight.shape, weight.dtype) for weight in weights],
        [FAR] * len(weights),
        [pltpu.SemaphoreType.DMA((2 * len(weights),))],
        0,
        4 * sum(weight.size for weight in weights),
    )(*weights)


def exchange_halves(values, lanes):
    half = RD // 2
    left = pltpu.roll(values, LANES - half, 1)
    right = pltpu.roll(values, half, 1)
    return jnp.where((lanes & half) == 0, left, right)


def norm_tiles(total, gain, out, start, count):
    tiles = [total[start + i * CHUNK : start + (i + 1) * CHUNK] for i in range(count)]
    squares = sum(tile * tile for tile in tiles)
    mean = jnp.sum(squares, axis=1, keepdims=True) * (1.0 / (count * LANES))
    factor = lax.rsqrt(mean + 1e-06)
    for index, tile in enumerate(tiles):
        out[start + index * CHUNK : start + (index + 1) * CHUNK] = (
            tile * factor * gain[index : index + 1, :]
        ).astype(out.dtype)


def norm_kernel(own, other, key_gain, query_gain, cosines, sines, out):
    total = own[...] + other[...]
    norm_tiles(total, key_gain, out, 0, KVL // LANES)
    norm_tiles(total, query_gain, out, PACK, QPACK)
    rope = total[KVL // LANES * CHUNK : PACK]
    lanes = lax.broadcasted_iota(jnp.int32, rope.shape, 1)
    out[KVL // LANES * CHUNK : PACK] = (
        rope * cosines[...] + exchange_halves(rope, lanes) * sines[...]
    ).astype(out.dtype)


def query_kernel(x_ref, piece0, piece1, piece2, piece3, up_query, up_key, cosines, sines, out, rows):
    pair = 2 * (NOPE + RD)
    pairs = up_query.shape[1] // pair
    for offset, piece in zip(OFFSETS, (piece0, piece1, piece2, piece3)):
        start = pl.multiple_of(((x_ref[0] + offset + NX) & (NX - 1)) * CHUNK, CHUNK)
        for tile in range(QPACK):
            rows[pl.ds(start, CHUNK), tile * LANES : (tile + 1) * LANES] = piece[
                PACK + tile * CHUNK : PACK + (tile + 1) * CHUNK
            ]
    tokens = rows.shape[0]
    lanes = lax.broadcasted_iota(jnp.int32, (tokens, LANES), 1)
    for index in range(pairs):
        full = jnp.dot(
            rows[...],
            up_query[:, index * pair : (index + 1) * pair],
            preferred_element_type=jnp.float32,
        )
        first, second, third = (full[:, i * LANES : (i + 1) * LANES] for i in range(3))
        second_half, third_half = pltpu.roll(second, RD, 1), pltpu.roll(third, RD, 1)
        heads = (
            (first, second),
            (jnp.where(lanes < RD, second_half, third_half), third_half),
        )
        for offset, (nope, rope) in enumerate(heads):
            head = 2 * index + offset
            absorbed = lax.dot_general(
                nope.astype(jnp.bfloat16),
                up_key[:, head * NOPE : (head + 1) * NOPE],
                CONTRACT_LAST,
                preferred_element_type=jnp.float32,
            )
            out[head * tokens : (head + 1) * tokens, :KVL] = absorbed.astype(out.dtype)
            turned = rope * cosines[...] + exchange_halves(rope, lanes) * sines[...]
            out[head * tokens : (head + 1) * tokens, KVL:] = jnp.where(
                lanes < RD, turned, 0.0
            ).astype(out.dtype)


def attend_kernel(parts, first, last, *refs):
    refs = list(refs)
    queries, key_at, query_at = refs[:3]
    sources, refs = refs[3 : 3 + parts], refs[3 + parts :]
    if not first:
        (old_top, old_total, old_acc), refs = refs[:3], refs[3:]
    if last:
        up_value, out, refs = refs[0], refs[1], refs[2:]
    else:
        (new_top, new_total, new_acc), refs = refs[:3], refs[3:]
    keys, scores, acc = refs

    chunks = TILE // CHUNK
    for part, source in enumerate(sources):
        for chunk in range(chunks):
            to, at = part * TILE + chunk * CHUNK, chunk * PACK
            for tile in range(KVL // LANES):
                keys[to : to + CHUNK, tile * LANES : (tile + 1) * LANES] = source[
                    at + tile * CHUNK : at + (tile + 1) * CHUNK
                ]
            rope = source[at + KVL // LANES * CHUNK : at + PACK]
            keys[to : to + CHUNK // 2, KVL:] = rope
            keys[to + CHUNK // 2 : to + CHUNK, KVL:] = jnp.concatenate(
                [rope[:, RD:], rope[:, :RD]], axis=1
            )

    tokens = query_at.shape[0]
    rows_at = jnp.concatenate([query_at[...]] * (SPAN // tokens), axis=0)
    spans = queries.shape[0] // SPAN
    tops, totals, weights = {}, {}, {}

    def score(span, tile):
        view = slice(tile * TILE, (tile + 1) * TILE)
        value = lax.dot_general(
            queries[span * SPAN : (span + 1) * SPAN],
            keys[view],
            CONTRACT_LAST,
            preferred_element_type=jnp.float32,
        )
        value = jnp.where(key_at[:, view] <= rows_at, value, NEG)
        scores[span % 2, :, view] = value
        for lane in range(TILE // LANES):
            column = value[:, lane * LANES : (lane + 1) * LANES]
            tops[span] = jnp.maximum(tops[span], column) if span in tops else column

    def mix(span, tile):
        rows = slice(span * SPAN, (span + 1) * SPAN)
        view = slice(tile * TILE, (tile + 1) * TILE)
        if tile == 0:
            top = jnp.max(tops[span], axis=1, keepdims=True)
            if not first:
                before = old_top[rows, :1]
                top = jnp.maximum(top, before)
                weights[span] = jnp.exp2((before - top) * (SCALE * LOG2E))
            tops[span] = top
        terms = jnp.exp2((scores[span % 2, :, view] - tops[span]) * (SCALE * LOG2E))
        for lane in range(TILE // LANES):
            column = terms[:, lane * LANES : (lane + 1) * LANES]
            totals[span] = totals[span] + column if span in totals else column
        value = jnp.dot(
            terms.astype(jnp.bfloat16), keys[view, :KVL], preferred_element_type=jnp.float32
        )
        if tile > 0:
            value = acc[span % 2] + value
        elif not first:
            value = old_acc[rows] * weights[span] + value
        if tile < parts - 1:
            acc[span % 2] = value
            return
        total = jnp.sum(totals[span], axis=1, keepdims=True)
        if not first:
            total = total + old_total[rows, :1] * weights[span]
        if not last:
            new_acc[rows] = value
            new_top[rows] = jnp.broadcast_to(tops[span], (SPAN, LANES))
            new_total[rows] = jnp.broadcast_to(total, (SPAN, LANES))
            return
        latent_mix = (value / total).astype(jnp.bfloat16)
        for index in range(SPAN // tokens):
            head = span * (SPAN // tokens) + index
            columns = slice(head * VD, (head + 1) * VD)
            out[:, columns] = jnp.dot(
                latent_mix[index * tokens : (index + 1) * tokens],
                up_value[:, columns],
                preferred_element_type=jnp.float32,
            ).astype(out.dtype)

    for span in range(spans + 1):
        for tile in range(parts):
            if span < spans:
                score(span, tile)
            if span > 0:
                mix(span - 1, tile)


def attend(queries, key_at, query_at, sources, state=(), up_value=None):
    rows, parts = queries.shape[0], len(sources)
    tokens = query_at.shape[0]
    if up_value is not None:
        out_shape = jax.ShapeDtypeStruct((tokens, rows // tokens * VD), jnp.bfloat16)
    else:
        out_shape = [
            jax.ShapeDtypeStruct((rows, LANES), jnp.float32),
            jax.ShapeDtypeStruct((rows, LANES), jnp.float32),
            jax.ShapeDtypeStruct((rows, KVL), jnp.float32),
        ]
    operands = [queries, key_at, query_at, *sources, *state]
    specs = [VMEM] * len(operands)
    keys = parts * TILE
    scratch = [
        pltpu.VMEM((keys, WIDE), jnp.bfloat16),
        pltpu.VMEM((2, SPAN, keys), jnp.float32),
        pltpu.VMEM((2, SPAN, KVL), jnp.float32),
    ]
    if up_value is not None:
        operands.append(up_value)
        specs.append(VMEM)
    return kernel_call(
        functools.partial(attend_kernel, parts, not state, up_value is not None),
        out_shape,
        specs,
        scratch,
        2 * rows * keys * (KVL + WIDE),
        keys * WIDE * 4,
    )(*operands)


def chunk_rows(x, y, zl, core):
    ring = jnp.array(OFFSETS, jnp.int32)
    first, second, third = ring[None, :, None], ring[:, None, None], ring[None, None, :]
    y_at = (y + jnp.where(core == 0, first, second)) % NY
    z_at = (zl + jnp.where(core == 0, second, first)) % NZL
    x_at = (x + third) % NX
    return (((z_at * NY + y_at) * NC + core) * (NX * CHUNK) + x_at * CHUNK).reshape(-1)


def body(
    hidden_states,
    down_query,
    down_latent,
    query_gain,
    latent_gain,
    up_query,
    up_key,
    up_value,
    owner_table,
):
    tok_rows = hidden_states.shape[0]
    local_heads = up_key.shape[1] // NOPE
    ctx = lax.axis_index("ctx")
    head = lax.axis_index("head")
    x = head % NX
    c, y, zl = ctx % NC, (ctx // NC) % NY, ctx // (NC * NY)
    x_index = x.reshape(1)

    firsts = jnp.concatenate([chunk_rows(x, y, zl, c), chunk_rows(x, y, zl, 1 - c)])
    starts = block_positions(owner_table, firsts, BLK)
    key_at = (starts[:, None] + jnp.arange(CHUNK, dtype=jnp.int32)[None, :]).reshape(1, -1)
    own_rows = ctx * tok_rows + jnp.arange(tok_rows, dtype=jnp.int32)
    own_positions = block_positions(owner_table, own_rows, BLK)
    key_cos, key_sin = (
        jnp.concatenate([table[: CHUNK // 2], table[CHUNK // 2 :]], axis=1)
        for table in rotary_tables(starts[0] + jnp.arange(CHUNK, dtype=jnp.int32))
    )
    query_cos, query_sin = (
        jnp.concatenate([table, table], axis=1) for table in rotary_tables(own_positions)
    )

    pieces = down(x_index, hidden_states, down_latent.T, down_query)
    arrived = [send(pieces[step], along_x(step)) for step in (1, 2, 3)]
    _, up_query, up_key, up_value = lax.optimization_barrier(
        (pieces[0], up_query, up_key, up_value)
    )
    arrived, tables, weights = lax.optimization_barrier(
        (
            arrived,
            (key_at, own_positions.reshape(-1, 1), key_cos, key_sin, query_cos, query_sin),
            load_weights(up_query, up_key, up_value),
        )
    )
    key_at, query_at, key_cos, key_sin, query_cos, query_sin = tables
    up_query, up_key, up_value = weights
    packed = pieces[0].shape
    half = kernel_call(
        sum_kernel,
        jax.ShapeDtypeStruct(packed, jnp.float32),
        [VMEM] * 4,
        [],
        4 * pieces[0].size,
        16 * pieces[0].size,
    )(pieces[0], *arrived)
    latents = kernel_call(
        norm_kernel,
        jax.ShapeDtypeStruct(packed, jnp.bfloat16),
        [VMEM] * 6,
        [],
        10 * half.size,
        10 * half.size,
    )(
        half,
        send(half, other_half),
        latent_gain.reshape(-1, LANES),
        query_gain.reshape(-1, LANES),
        key_cos,
        key_sin,
    )
    pieces = gather_ring(latents, along_x)
    key_own = join(pieces, PACK)
    key_first = join(gather_ring(key_own, along_first), key_own.shape[0])

    queries = kernel_call(
        query_kernel,
        jax.ShapeDtypeStruct((local_heads * tok_rows, WIDE), jnp.bfloat16),
        [SMEM] + [VMEM] * 8,
        [pltpu.VMEM((tok_rows, up_query.shape[0]), jnp.bfloat16)],
        2 * tok_rows * (up_query.size + up_key.size),
        2 * (up_query.size + up_key.size),
        limit=16,
    )(x_index, *pieces, up_query, up_key, query_cos, query_sin)

    near = gather_ring(key_first, along_second)
    key_parts = [key_at[:, part * TILE : (part + 1) * TILE] for part in range(2 * len(near))]

    def stage(sources, places, state, last=False):
        return attend(
            queries,
            jnp.concatenate([key_parts[place] for place in places], axis=1),
            query_at,
            sources,
            state,
            up_value if last else None,
        )

    state = stage([near[0]], [0], ())
    near[:3], state = lax.optimization_barrier((near[:3], state))
    far = [send(part, other_core) for part in near[:3]]
    state = stage([near[1], near[2]], [1, 2], state)
    near[3], state = lax.optimization_barrier((near[3], state))
    far.append(send(near[3], other_core))
    state = stage([near[3]], [3], state)
    return stage(far, [4, 5, 6, 7], state, last=True)


def solution(mesh):
    placed = (
        P("ctx", "head"),
        P("head", None),
        P("head", None),
        P(),
        P(),
        P(None, "head"),
        P(None, "head"),
        P(None, "head"),
        P(),
    )
    return jax.shard_map(
        body, mesh=mesh, in_specs=placed, out_specs=P("ctx", "head"), check_vma=False
    )
```

```python
import functools
import math

import jax
import jax.numpy as jnp
from jax import lax
from jax.experimental import pallas as pl
from jax.experimental.pallas import tpu as pltpu
from jax.sharding import PartitionSpec as P

RD = 64
NOPE = 128
VD = 128
KVL = 512
BLK = 64
LANES = 128
WIDE = KVL + LANES
CHUNK = 32
PACK = CHUNK * (KVL + RD) // LANES
QPACK = 12
TILE = 512
SPAN = 256
NEG = -1e30
SCALE = 1.0 / math.sqrt(NOPE + RD)
LOG2E = math.log2(math.e)
NX, NY, NZ, NZL, NC = 4, 4, 8, 4, 2
AXES = ("ctx", "head")
OFFSETS = (0, -1, 1, 2)
CONTRACT_LAST = (((1,), (1,)), ((), ()))
VMEM = pl.BlockSpec(memory_space=pltpu.VMEM)
SMEM = pl.BlockSpec(memory_space=pltpu.SMEM)
FAR = pl.BlockSpec(memory_space=pltpu.HBM)


def angles(positions):
    half_width = RD // 2
    step_index = jnp.arange(half_width).astype(jnp.float32)
    frequency = jnp.exp(step_index * (-math.log(10000.0) / half_width))
    return positions.astype(jnp.float32)[..., None] * frequency


def rotary_tables(positions):
    table = angles(positions)
    cosines, sines = jnp.cos(table), jnp.sin(table)
    return (
        jnp.concatenate([cosines, cosines], axis=-1),
        jnp.concatenate([-sines, sines], axis=-1),
    )


def block_positions(owner_table, row_index, block_rows):
    slot_index = row_index // block_rows
    block_count = owner_table.shape[0]
    match_table = (owner_table[None, :] == slot_index[:, None]).astype(jnp.int32)
    block_index = jnp.sum(match_table * jnp.arange(block_count, dtype=jnp.int32)[None, :], axis=1)
    return block_index * block_rows + row_index % block_rows


def flat(x, y, z, c):
    ctx = ((z % NZL) * NY + y) * NC + c
    return ctx * (2 * NX) + (z // NZL) * NX + x


def send(value, move):
    pairs = []
    for x in range(NX):
        for y in range(NY):
            for z in range(NZ):
                for c in range(NC):
                    tx, ty, tz, tc = move(x, y, z, c)
                    pairs.append((flat(x, y, z, c), flat(tx % NX, ty % NY, tz % NZ, tc)))
    return lax.ppermute(value, AXES, pairs)


def along_x(step):
    return lambda x, y, z, c: (x + step, y, z, c)


def pair_x(shift):
    return lambda x, y, z, c: (x + (1 if (x + shift) % 2 == 0 else -1), y, z, c)


def pair_order(x):
    partner = (x + NX - 1 + 2 * (x & 1)) & (NX - 1)
    return [x, x + 1 - 2 * (x & 1), partner, partner + 1 - 2 * (partner & 1)]


def step_z(z, step):
    return z - step if abs(step) == 2 and z % 2 else z + step


def along_first(step):
    return lambda x, y, z, c: (x, y + step, z, c) if c == 0 else (x, y, step_z(z, step), c)


def along_second(step):
    return lambda x, y, z, c: (x, y, step_z(z, step), c) if c == 0 else (x, y + step, z, c)


def other_half(x, y, z, c):
    return (x, y, z + NZL, c)


def other_core(x, y, z, c):
    return (x, y, z, 1 - c)


def gather_ring(value, along):
    return [value] + [send(value, along(-offset)) for offset in OFFSETS[1:]]


def kernel_call(kernel, out_shape, in_specs, scratch, flops, moved, limit=32):
    return pl.pallas_call(
        kernel,
        out_shape=out_shape,
        in_specs=in_specs,
        out_specs=jax.tree.map(lambda _: VMEM, out_shape),
        scratch_shapes=scratch,
        compiler_params=pltpu.CompilerParams(vmem_limit_bytes=limit * 2**20),
        cost_estimate=pl.CostEstimate(flops=flops, bytes_accessed=moved, transcendentals=0),
    )


def key_down_kernel(x_ref, hidden_far, weight_far, *refs):
    pieces, (hidden, weight, part, sems) = refs[:NX], refs[NX:]
    half = weight.shape[0] // 2
    loads = [pltpu.make_async_copy(hidden_far, hidden, sems.at[0])]
    for index in range(2):
        rows = pl.ds(index * half, half)
        loads.append(
            pltpu.make_async_copy(weight_far.at[rows], weight.at[rows], sems.at[1 + index])
        )
    for load in loads:
        load.start()
    for load in loads:
        load.wait()
    part[...] = lax.dot_general(
        hidden[...], weight[...], CONTRACT_LAST, preferred_element_type=jnp.float32
    )
    for step, piece in enumerate(pieces):
        start = pl.multiple_of(((x_ref[0] + step) & (NX - 1)) * CHUNK, CHUNK)
        rows = part[pl.ds(start, CHUNK), :]
        for tile in range(KVL // LANES):
            piece[tile * CHUNK : (tile + 1) * CHUNK] = rows[:, tile * LANES : (tile + 1) * LANES]
        rope = rows[:, KVL:]
        piece[KVL // LANES * CHUNK : PACK] = jnp.concatenate(
            [rope[: CHUNK // 2], rope[CHUNK // 2 :]], axis=1
        )


def key_down(x_index, hidden, weight):
    rows = hidden.shape[0]
    return kernel_call(
        key_down_kernel,
        [jax.ShapeDtypeStruct((PACK, LANES), jnp.float32)] * NX,
        [SMEM, FAR, FAR],
        [
            pltpu.VMEM(hidden.shape, hidden.dtype),
            pltpu.VMEM(weight.shape, weight.dtype),
            pltpu.VMEM((rows, weight.shape[0]), jnp.float32),
            pltpu.SemaphoreType.DMA((3,)),
        ],
        2 * rows * weight.size,
        2 * weight.size,
        limit=63,
    )(x_index, hidden, weight)


def query_down_kernel(x_ref, hidden, weight, *refs):
    pieces, part = refs[:NX], refs[NX]
    part[...] = jnp.dot(hidden[...], weight[...], preferred_element_type=jnp.float32)
    for step, piece in enumerate(pieces):
        start = pl.multiple_of(((x_ref[0] + step) & (NX - 1)) * CHUNK, CHUNK)
        for tile in range(QPACK):
            piece[tile * CHUNK : (tile + 1) * CHUNK] = part[
                pl.ds(start, CHUNK), tile * LANES : (tile + 1) * LANES
            ]


def query_down(x_index, hidden, weight):
    rows = hidden.shape[0]
    return kernel_call(
        query_down_kernel,
        [jax.ShapeDtypeStruct((QPACK * CHUNK, LANES), jnp.float32)] * NX,
        [SMEM, VMEM, VMEM],
        [pltpu.VMEM((rows, weight.shape[1]), jnp.float32)],
        2 * rows * weight.size,
        2 * weight.size,
        limit=16,
    )(x_index, hidden, weight)


def sum_kernel(own, one, two, three, out):
    out[...] = own[...] + one[...] + two[...] + three[...]


def reduce_x(pieces):
    arrived = [send(pieces[step], along_x(step)) for step in (1, 2, 3)]
    return kernel_call(
        sum_kernel,
        jax.ShapeDtypeStruct(pieces[0].shape, jnp.float32),
        [VMEM] * 4,
        [],
        4 * pieces[0].size,
        16 * pieces[0].size,
    )(pieces[0], *arrived)


def join_kernel(rows, *refs):
    pieces, out = refs[:-1], refs[-1]
    for index, piece in enumerate(pieces):
        out[index * rows : (index + 1) * rows] = piece[:rows]


def join(pieces, rows):
    shape = (len(pieces) * rows, LANES)
    size = len(pieces) * rows * LANES
    return kernel_call(
        functools.partial(join_kernel, rows),
        jax.ShapeDtypeStruct(shape, pieces[0].dtype),
        [VMEM] * len(pieces),
        [],
        size,
        4 * size,
    )(*pieces)


def exchange_halves(values, lanes):
    half = RD // 2
    left = pltpu.roll(values, LANES - half, 1)
    right = pltpu.roll(values, half, 1)
    return jnp.where((lanes & half) == 0, left, right)


def norm_tiles(total, gain, out, start, count):
    tiles = [total[start + i * CHUNK : start + (i + 1) * CHUNK] for i in range(count)]
    squares = sum(tile * tile for tile in tiles)
    mean = jnp.sum(squares, axis=1, keepdims=True) * (1.0 / (count * LANES))
    factor = lax.rsqrt(mean + 1e-06)
    for index, tile in enumerate(tiles):
        out[start + index * CHUNK : start + (index + 1) * CHUNK] = (
            tile * factor * gain[index : index + 1, :]
        ).astype(out.dtype)


def key_norm_kernel(own, other, gain, cosines, sines, out):
    total = own[...] + other[...]
    norm_tiles(total, gain, out, 0, KVL // LANES)
    rope = total[KVL // LANES * CHUNK :]
    lanes = lax.broadcasted_iota(jnp.int32, rope.shape, 1)
    out[KVL // LANES * CHUNK :] = (
        rope * cosines[...] + exchange_halves(rope, lanes) * sines[...]
    ).astype(out.dtype)


def query_norm_kernel(own, other, gain, out):
    norm_tiles(own[...] + other[...], gain, out, 0, QPACK)


def query_kernel(x_ref, own, first, second, up_query, up_key, cosines, sines, out, rows):
    pair = 2 * (NOPE + RD)
    pairs = up_query.shape[1] // pair
    size = QPACK * CHUNK
    places = zip(pair_order(x_ref[0]), (own, first, second, second), (0, 0, 0, size))
    for place, piece, at in places:
        start = pl.multiple_of(place * CHUNK, CHUNK)
        for tile in range(QPACK):
            rows[pl.ds(start, CHUNK), tile * LANES : (tile + 1) * LANES] = piece[
                at + tile * CHUNK : at + (tile + 1) * CHUNK
            ]
    tokens = rows.shape[0]
    lanes = lax.broadcasted_iota(jnp.int32, (tokens, LANES), 1)
    for index in range(pairs):
        full = jnp.dot(
            rows[...],
            up_query[:, index * pair : (index + 1) * pair],
            preferred_element_type=jnp.float32,
        )
        first, second, third = (full[:, i * LANES : (i + 1) * LANES] for i in range(3))
        second_half, third_half = pltpu.roll(second, RD, 1), pltpu.roll(third, RD, 1)
        heads = (
            (first, second),
            (jnp.where(lanes < RD, second_half, third_half), third_half),
        )
        for offset, (nope, rope) in enumerate(heads):
            head = 2 * index + offset
            absorbed = lax.dot_general(
                nope.astype(jnp.bfloat16),
                up_key[:, head * NOPE : (head + 1) * NOPE],
                CONTRACT_LAST,
                preferred_element_type=jnp.float32,
            )
            out[head * tokens : (head + 1) * tokens, :KVL] = absorbed.astype(out.dtype)
            turned = rope * cosines[...] + exchange_halves(rope, lanes) * sines[...]
            out[head * tokens : (head + 1) * tokens, KVL:] = jnp.where(
                lanes < RD, turned, 0.0
            ).astype(out.dtype)


def attend_kernel(parts, first, last, *refs):
    refs = list(refs)
    queries, key_at, query_at = refs[:3]
    sources, refs = refs[3 : 3 + parts], refs[3 + parts :]
    if not first:
        (old_top, old_total, old_acc), refs = refs[:3], refs[3:]
    if last:
        up_value, out, refs = refs[0], refs[1], refs[2:]
    else:
        (new_top, new_total, new_acc), refs = refs[:3], refs[3:]
    keys, scores, acc = refs

    chunks = TILE // CHUNK
    for part, source in enumerate(sources):
        for chunk in range(chunks):
            to, at = part * TILE + chunk * CHUNK, chunk * PACK
            for tile in range(KVL // LANES):
                keys[to : to + CHUNK, tile * LANES : (tile + 1) * LANES] = source[
                    at + tile * CHUNK : at + (tile + 1) * CHUNK
                ]
            rope = source[at + KVL // LANES * CHUNK : at + PACK]
            keys[to : to + CHUNK // 2, KVL:] = rope
            keys[to + CHUNK // 2 : to + CHUNK, KVL:] = jnp.concatenate(
                [rope[:, RD:], rope[:, :RD]], axis=1
            )

    tokens = query_at.shape[0]
    rows_at = jnp.concatenate([query_at[...]] * (SPAN // tokens), axis=0)
    spans = queries.shape[0] // SPAN
    tops, totals, weights = {}, {}, {}

    def score(span, tile):
        view = slice(tile * TILE, (tile + 1) * TILE)
        value = lax.dot_general(
            queries[span * SPAN : (span + 1) * SPAN],
            keys[view],
            CONTRACT_LAST,
            preferred_element_type=jnp.float32,
        )
        value = jnp.where(key_at[:, view] <= rows_at, value, NEG)
        scores[span % 2, :, view] = value
        for lane in range(TILE // LANES):
            column = value[:, lane * LANES : (lane + 1) * LANES]
            tops[span] = jnp.maximum(tops[span], column) if span in tops else column

    def mix(span, tile):
        rows = slice(span * SPAN, (span + 1) * SPAN)
        view = slice(tile * TILE, (tile + 1) * TILE)
        if tile == 0:
            top = jnp.max(tops[span], axis=1, keepdims=True)
            if not first:
                before = old_top[rows, :1]
                top = jnp.maximum(top, before)
                weights[span] = jnp.exp2((before - top) * (SCALE * LOG2E))
            tops[span] = top
        terms = jnp.exp2((scores[span % 2, :, view] - tops[span]) * (SCALE * LOG2E))
        for lane in range(TILE // LANES):
            column = terms[:, lane * LANES : (lane + 1) * LANES]
            totals[span] = totals[span] + column if span in totals else column
        value = jnp.dot(
            terms.astype(jnp.bfloat16), keys[view, :KVL], preferred_element_type=jnp.float32
        )
        if tile > 0:
            value = acc[span % 2] + value
        elif not first:
            value = old_acc[rows] * weights[span] + value
        if tile < parts - 1:
            acc[span % 2] = value
            return
        total = jnp.sum(totals[span], axis=1, keepdims=True)
        if not first:
            total = total + old_total[rows, :1] * weights[span]
        if not last:
            new_acc[rows] = value
            new_top[rows] = jnp.broadcast_to(tops[span], (SPAN, LANES))
            new_total[rows] = jnp.broadcast_to(total, (SPAN, LANES))
            return
        latent_mix = (value / total).astype(jnp.bfloat16)
        for index in range(SPAN // tokens):
            head = span * (SPAN // tokens) + index
            columns = slice(head * VD, (head + 1) * VD)
            out[:, columns] = jnp.dot(
                latent_mix[index * tokens : (index + 1) * tokens],
                up_value[:, columns],
                preferred_element_type=jnp.float32,
            ).astype(out.dtype)

    for span in range(spans + 1):
        for tile in range(parts):
            if span < spans:
                score(span, tile)
            if span > 0:
                mix(span - 1, tile)


def attend(queries, key_at, query_at, sources, state=(), up_value=None):
    rows, parts = queries.shape[0], len(sources)
    tokens = query_at.shape[0]
    if up_value is not None:
        out_shape = jax.ShapeDtypeStruct((tokens, rows // tokens * VD), jnp.bfloat16)
    else:
        out_shape = [
            jax.ShapeDtypeStruct((rows, LANES), jnp.float32),
            jax.ShapeDtypeStruct((rows, LANES), jnp.float32),
            jax.ShapeDtypeStruct((rows, KVL), jnp.float32),
        ]
    operands = [queries, key_at, query_at, *sources, *state]
    specs = [VMEM] * len(operands)
    keys = parts * TILE
    scratch = [
        pltpu.VMEM((keys, WIDE), jnp.bfloat16),
        pltpu.VMEM((2, SPAN, keys), jnp.float32),
        pltpu.VMEM((2, SPAN, KVL), jnp.float32),
    ]
    if up_value is not None:
        operands.append(up_value)
        specs.append(VMEM)
    return kernel_call(
        functools.partial(attend_kernel, parts, not state, up_value is not None),
        out_shape,
        specs,
        scratch,
        2 * rows * keys * (KVL + WIDE),
        keys * WIDE * 4,
    )(*operands)


def chunk_rows(x, y, zl, core):
    ring = jnp.array(OFFSETS, jnp.int32)
    first, second = ring[None, :, None], ring[:, None, None]
    y_at = (y + jnp.where(core == 0, first, second)) % NY
    z_at = (zl + jnp.where(core == 0, second, first)) % NZL
    x_at = jnp.stack(pair_order(x))[None, None, :]
    return (((z_at * NY + y_at) * NC + core) * (NX * CHUNK) + x_at * CHUNK).reshape(-1)


def body(
    hidden_states,
    down_query,
    down_latent,
    query_gain,
    latent_gain,
    up_query,
    up_key,
    up_value,
    owner_table,
):
    tok_rows = hidden_states.shape[0]
    local_heads = up_key.shape[1] // NOPE
    ctx = lax.axis_index("ctx")
    head = lax.axis_index("head")
    x = head % NX
    c, y, zl = ctx % NC, (ctx // NC) % NY, ctx // (NC * NY)
    x_index = x.reshape(1)

    firsts = jnp.concatenate([chunk_rows(x, y, zl, c), chunk_rows(x, y, zl, 1 - c)])
    starts = block_positions(owner_table, firsts, BLK)
    key_at = (starts[:, None] + jnp.arange(CHUNK, dtype=jnp.int32)[None, :]).reshape(1, -1)
    own_rows = ctx * tok_rows + jnp.arange(tok_rows, dtype=jnp.int32)
    own_positions = block_positions(owner_table, own_rows, BLK)
    key_cos, key_sin = (
        jnp.concatenate([table[: CHUNK // 2], table[CHUNK // 2 :]], axis=1)
        for table in rotary_tables(starts[0] + jnp.arange(CHUNK, dtype=jnp.int32))
    )
    query_cos, query_sin = (
        jnp.concatenate([table, table], axis=1) for table in rotary_tables(own_positions)
    )

    key_half = reduce_x(key_down(x_index, hidden_states, down_latent.T))
    key_other = send(key_half, other_half)
    _, hidden_states = lax.optimization_barrier((key_half, hidden_states))
    query_pieces = query_down(x_index, hidden_states, down_query)
    key_pack = kernel_call(
        key_norm_kernel,
        jax.ShapeDtypeStruct((PACK, LANES), jnp.bfloat16),
        [VMEM] * 5,
        [],
        10 * PACK * LANES,
        10 * PACK * LANES,
    )(key_half, key_other, latent_gain.reshape(-1, LANES), key_cos, key_sin)
    key_pack, query_pieces = lax.optimization_barrier((key_pack, query_pieces))
    query_half = reduce_x(query_pieces)
    key_pair = join([key_pack, send(key_pack, pair_x(0))], PACK)
    key_own = join([key_pair, send(key_pair, pair_x(1))], 2 * PACK)
    key_own, query_half = lax.optimization_barrier((key_own, query_half))
    key_first = join(gather_ring(key_own, along_first), key_own.shape[0])

    query_rows = QPACK * CHUNK
    query_latent = kernel_call(
        query_norm_kernel,
        jax.ShapeDtypeStruct(query_half.shape, jnp.bfloat16),
        [VMEM] * 3,
        [],
        10 * query_half.size,
        10 * query_half.size,
    )(query_half, send(query_half, other_half), query_gain.reshape(-1, LANES))
    query_first = send(query_latent, pair_x(0))
    query_second = send(join([query_latent, query_first], query_rows), pair_x(1))
    queries = kernel_call(
        query_kernel,
        jax.ShapeDtypeStruct((local_heads * tok_rows, WIDE), jnp.bfloat16),
        [SMEM] + [VMEM] * 7,
        [pltpu.VMEM((tok_rows, up_query.shape[0]), jnp.bfloat16)],
        2 * tok_rows * (up_query.size + up_key.size),
        2 * (up_query.size + up_key.size),
        limit=16,
    )(x_index, query_latent, query_first, query_second, up_query, up_key, query_cos, query_sin)

    near = gather_ring(key_first, along_second)
    key_parts = [key_at[:, part * TILE : (part + 1) * TILE] for part in range(2 * len(near))]

    query_at = own_positions.reshape(-1, 1)

    def stage(sources, places, state, last=False):
        return attend(
            queries,
            jnp.concatenate([key_parts[place] for place in places], axis=1),
            query_at,
            sources,
            state,
            up_value if last else None,
        )

    state = stage([near[0]], [0], ())
    near[:3], state = lax.optimization_barrier((near[:3], state))
    far = [send(part, other_core) for part in near[:3]]
    state = stage([near[1], near[2]], [1, 2], state)
    near[3], state = lax.optimization_barrier((near[3], state))
    far.append(send(near[3], other_core))
    state = stage(far[:3], [4, 5, 6], state)
    return stage([near[3], far[3]], [3, 7], state, last=True)


def solution(mesh):
    placed = (
        P("ctx", "head"),
        P("head", None),
        P("head", None),
        P(),
        P(),
        P(None, "head"),
        P(None, "head"),
        P(None, "head"),
        P(),
    )
    return jax.shard_map(
        body, mesh=mesh, in_specs=placed, out_specs=P("ctx", "head"), check_vma=False
    )
```

```python
import functools
import math

import jax
import jax.numpy as jnp
from jax import lax
from jax.experimental import pallas as pl
from jax.experimental.pallas import tpu as pltpu
from jax.sharding import PartitionSpec as P

RD = 64
NOPE = 128
VD = 128
KVL = 512
BLK = 64
LANES = 128
WIDE = KVL + LANES
CHUNK = 32
PACK = CHUNK * (KVL + RD) // LANES
QPACK = 12
TILE = 512
SPAN = 256
NEG = -1e30
SCALE = 1.0 / math.sqrt(NOPE + RD)
LOG2E = math.log2(math.e)
NX, NY, NZ, NZL, NC = 4, 4, 8, 4, 2
AXES = ("ctx", "head")
OFFSETS = (0, -1, 1, 2)
CONTRACT_LAST = (((1,), (1,)), ((), ()))
VMEM = pl.BlockSpec(memory_space=pltpu.VMEM)
SMEM = pl.BlockSpec(memory_space=pltpu.SMEM)
FAR = pl.BlockSpec(memory_space=pltpu.HBM)


def angles(positions):
    half_width = RD // 2
    step_index = jnp.arange(half_width).astype(jnp.float32)
    frequency = jnp.exp(step_index * (-math.log(10000.0) / half_width))
    return positions.astype(jnp.float32)[..., None] * frequency


def rotary_tables(positions):
    table = angles(positions)
    cosines, sines = jnp.cos(table), jnp.sin(table)
    return (
        jnp.concatenate([cosines, cosines], axis=-1),
        jnp.concatenate([-sines, sines], axis=-1),
    )


def block_positions(owner_table, row_index, block_rows):
    slot_index = row_index // block_rows
    block_count = owner_table.shape[0]
    match_table = (owner_table[None, :] == slot_index[:, None]).astype(jnp.int32)
    block_index = jnp.sum(match_table * jnp.arange(block_count, dtype=jnp.int32)[None, :], axis=1)
    return block_index * block_rows + row_index % block_rows


def flat(x, y, z, c):
    ctx = ((z % NZL) * NY + y) * NC + c
    return ctx * (2 * NX) + (z // NZL) * NX + x


def send(value, move):
    pairs = []
    for x in range(NX):
        for y in range(NY):
            for z in range(NZ):
                for c in range(NC):
                    tx, ty, tz, tc = move(x, y, z, c)
                    pairs.append((flat(x, y, z, c), flat(tx % NX, ty % NY, tz % NZ, tc)))
    return lax.ppermute(value, AXES, pairs)


def along_x(step):
    return lambda x, y, z, c: (x + step, y, z, c)


def pair_x(shift):
    return lambda x, y, z, c: (x + (1 if (x + shift) % 2 == 0 else -1), y, z, c)


def pair_order(x):
    partner = (x + NX - 1 + 2 * (x & 1)) & (NX - 1)
    return [x, x + 1 - 2 * (x & 1), partner, partner + 1 - 2 * (partner & 1)]


def step_z(z, step):
    return z - step if abs(step) == 2 and z % 2 else z + step


def along_first(step):
    return lambda x, y, z, c: (x, y + step, z, c) if c == 0 else (x, y, step_z(z, step), c)


def along_second(step):
    return lambda x, y, z, c: (x, y, step_z(z, step), c) if c == 0 else (x, y + step, z, c)


def other_half(x, y, z, c):
    return (x, y, z + NZL, c)


def other_core(x, y, z, c):
    return (x, y, z, 1 - c)


def gather_ring(value, along):
    return [value] + [send(value, along(-offset)) for offset in OFFSETS[1:]]


def kernel_call(kernel, out_shape, in_specs, scratch, flops, moved, limit=32):
    return pl.pallas_call(
        kernel,
        out_shape=out_shape,
        in_specs=in_specs,
        out_specs=jax.tree.map(lambda _: VMEM, out_shape),
        scratch_shapes=scratch,
        compiler_params=pltpu.CompilerParams(vmem_limit_bytes=limit * 2**20),
        cost_estimate=pl.CostEstimate(flops=flops, bytes_accessed=moved, transcendentals=0),
    )


def key_down_kernel(x_ref, hidden_far, weight_far, *refs):
    pieces, (hidden, weight, part, sems) = refs[:NX], refs[NX:]
    half = weight.shape[0] // 2
    loads = [pltpu.make_async_copy(hidden_far, hidden, sems.at[0])]
    for index in range(2):
        rows = pl.ds(index * half, half)
        loads.append(
            pltpu.make_async_copy(weight_far.at[rows], weight.at[rows], sems.at[1 + index])
        )
    for load in loads:
        load.start()
    for load in loads:
        load.wait()
    part[...] = lax.dot_general(
        hidden[...], weight[...], CONTRACT_LAST, preferred_element_type=jnp.float32
    )
    for step, piece in enumerate(pieces):
        start = pl.multiple_of(((x_ref[0] + step) & (NX - 1)) * CHUNK, CHUNK)
        rows = part[pl.ds(start, CHUNK), :]
        for tile in range(KVL // LANES):
            piece[tile * CHUNK : (tile + 1) * CHUNK] = rows[:, tile * LANES : (tile + 1) * LANES]
        rope = rows[:, KVL:]
        piece[KVL // LANES * CHUNK : PACK] = jnp.concatenate(
            [rope[: CHUNK // 2], rope[CHUNK // 2 :]], axis=1
        )


def key_down(x_index, hidden, weight):
    rows = hidden.shape[0]
    return kernel_call(
        key_down_kernel,
        [jax.ShapeDtypeStruct((PACK, LANES), jnp.float32)] * NX,
        [SMEM, FAR, FAR],
        [
            pltpu.VMEM(hidden.shape, hidden.dtype),
            pltpu.VMEM(weight.shape, weight.dtype),
            pltpu.VMEM((rows, weight.shape[0]), jnp.float32),
            pltpu.SemaphoreType.DMA((3,)),
        ],
        2 * rows * weight.size,
        2 * weight.size,
        limit=63,
    )(x_index, hidden, weight)


def query_down_kernel(x_ref, hidden, weight, *refs):
    pieces, part = refs[:NX], refs[NX]
    part[...] = jnp.dot(hidden[...], weight[...], preferred_element_type=jnp.float32)
    for step, piece in enumerate(pieces):
        start = pl.multiple_of(((x_ref[0] + step) & (NX - 1)) * CHUNK, CHUNK)
        for tile in range(QPACK):
            piece[tile * CHUNK : (tile + 1) * CHUNK] = part[
                pl.ds(start, CHUNK), tile * LANES : (tile + 1) * LANES
            ]


def query_down(x_index, hidden, weight):
    rows = hidden.shape[0]
    return kernel_call(
        query_down_kernel,
        [jax.ShapeDtypeStruct((QPACK * CHUNK, LANES), jnp.float32)] * NX,
        [SMEM, VMEM, VMEM],
        [pltpu.VMEM((rows, weight.shape[1]), jnp.float32)],
        2 * rows * weight.size,
        2 * weight.size,
        limit=16,
    )(x_index, hidden, weight)


def sum_kernel(own, one, two, three, out):
    out[...] = own[...] + one[...] + two[...] + three[...]


def reduce_x(pieces):
    arrived = [send(pieces[step], along_x(step)) for step in (1, 2, 3)]
    return kernel_call(
        sum_kernel,
        jax.ShapeDtypeStruct(pieces[0].shape, jnp.float32),
        [VMEM] * 4,
        [],
        4 * pieces[0].size,
        16 * pieces[0].size,
    )(pieces[0], *arrived)


def join_kernel(rows, *refs):
    pieces, out = refs[:-1], refs[-1]
    for index, piece in enumerate(pieces):
        out[index * rows : (index + 1) * rows] = piece[:rows]


def join(pieces, rows):
    shape = (len(pieces) * rows, LANES)
    size = len(pieces) * rows * LANES
    return kernel_call(
        functools.partial(join_kernel, rows),
        jax.ShapeDtypeStruct(shape, pieces[0].dtype),
        [VMEM] * len(pieces),
        [],
        size,
        4 * size,
    )(*pieces)


def exchange_halves(values, lanes):
    half = RD // 2
    left = pltpu.roll(values, LANES - half, 1)
    right = pltpu.roll(values, half, 1)
    return jnp.where((lanes & half) == 0, left, right)


def norm_tiles(total, gain, out, start, count):
    tiles = [total[start + i * CHUNK : start + (i + 1) * CHUNK] for i in range(count)]
    squares = sum(tile * tile for tile in tiles)
    mean = jnp.sum(squares, axis=1, keepdims=True) * (1.0 / (count * LANES))
    factor = lax.rsqrt(mean + 1e-06)
    for index, tile in enumerate(tiles):
        out[start + index * CHUNK : start + (index + 1) * CHUNK] = (
            tile * factor * gain[index : index + 1, :]
        ).astype(out.dtype)


def key_norm_kernel(own, other, gain, cosines, sines, out):
    total = own[...] + other[...]
    norm_tiles(total, gain, out, 0, KVL // LANES)
    rope = total[KVL // LANES * CHUNK :]
    lanes = lax.broadcasted_iota(jnp.int32, rope.shape, 1)
    out[KVL // LANES * CHUNK :] = (
        rope * cosines[...] + exchange_halves(rope, lanes) * sines[...]
    ).astype(out.dtype)


def query_norm_kernel(own, other, gain, out):
    norm_tiles(own[...] + other[...], gain, out, 0, QPACK)


def query_kernel(x_ref, own, first, second, up_query, up_key, cosines, sines, out, rows):
    pair = 2 * (NOPE + RD)
    pairs = up_query.shape[1] // pair
    size = QPACK * CHUNK
    places = zip(pair_order(x_ref[0]), (own, first, second, second), (0, 0, 0, size))
    for place, piece, at in places:
        start = pl.multiple_of(place * CHUNK, CHUNK)
        for tile in range(QPACK):
            rows[pl.ds(start, CHUNK), tile * LANES : (tile + 1) * LANES] = piece[
                at + tile * CHUNK : at + (tile + 1) * CHUNK
            ]
    tokens = rows.shape[0]
    lanes = lax.broadcasted_iota(jnp.int32, (tokens, LANES), 1)
    for index in range(pairs):
        full = jnp.dot(
            rows[...],
            up_query[:, index * pair : (index + 1) * pair],
            preferred_element_type=jnp.float32,
        )
        first, second, third = (full[:, i * LANES : (i + 1) * LANES] for i in range(3))
        second_half, third_half = pltpu.roll(second, RD, 1), pltpu.roll(third, RD, 1)
        heads = (
            (first, second),
            (jnp.where(lanes < RD, second_half, third_half), third_half),
        )
        for offset, (nope, rope) in enumerate(heads):
            head = 2 * index + offset
            absorbed = lax.dot_general(
                nope.astype(jnp.bfloat16),
                up_key[:, head * NOPE : (head + 1) * NOPE],
                CONTRACT_LAST,
                preferred_element_type=jnp.float32,
            )
            out[head * tokens : (head + 1) * tokens, :KVL] = absorbed.astype(out.dtype)
            turned = rope * cosines[...] + exchange_halves(rope, lanes) * sines[...]
            out[head * tokens : (head + 1) * tokens, KVL:] = jnp.where(
                lanes < RD, turned, 0.0
            ).astype(out.dtype)


def attend_kernel(parts, first, last, *refs):
    refs = list(refs)
    queries, key_at, query_at = refs[:3]
    sources, refs = refs[3 : 3 + parts], refs[3 + parts :]
    if not first:
        (old_top, old_total, old_acc), refs = refs[:3], refs[3:]
    if last:
        up_value, out, refs = refs[0], refs[1], refs[2:]
    else:
        (new_top, new_total, new_acc), refs = refs[:3], refs[3:]
    keys, scores, acc = refs

    chunks = TILE // CHUNK
    for part, source in enumerate(sources):
        for chunk in range(chunks):
            to, at = part * TILE + chunk * CHUNK, chunk * PACK
            for tile in range(KVL // LANES):
                keys[to : to + CHUNK, tile * LANES : (tile + 1) * LANES] = source[
                    at + tile * CHUNK : at + (tile + 1) * CHUNK
                ]
            rope = source[at + KVL // LANES * CHUNK : at + PACK]
            keys[to : to + CHUNK // 2, KVL:] = rope
            keys[to + CHUNK // 2 : to + CHUNK, KVL:] = jnp.concatenate(
                [rope[:, RD:], rope[:, :RD]], axis=1
            )

    tokens = query_at.shape[0]
    rows_at = jnp.concatenate([query_at[...]] * (SPAN // tokens), axis=0)
    spans = queries.shape[0] // SPAN
    tops, totals, weights = {}, {}, {}

    def score(span, tile):
        view = slice(tile * TILE, (tile + 1) * TILE)
        value = lax.dot_general(
            queries[span * SPAN : (span + 1) * SPAN],
            keys[view],
            CONTRACT_LAST,
            preferred_element_type=jnp.float32,
        )
        value = jnp.where(key_at[:, view] <= rows_at, value, NEG)
        scores[span % 2, :, view] = value
        for lane in range(TILE // LANES):
            column = value[:, lane * LANES : (lane + 1) * LANES]
            tops[span] = jnp.maximum(tops[span], column) if span in tops else column

    def mix(span, tile):
        rows = slice(span * SPAN, (span + 1) * SPAN)
        view = slice(tile * TILE, (tile + 1) * TILE)
        if tile == 0:
            top = jnp.max(tops[span], axis=1, keepdims=True)
            if not first:
                before = old_top[rows, :1]
                top = jnp.maximum(top, before)
                weights[span] = jnp.exp2((before - top) * (SCALE * LOG2E))
            tops[span] = top
        terms = jnp.exp2((scores[span % 2, :, view] - tops[span]) * (SCALE * LOG2E))
        for lane in range(TILE // LANES):
            column = terms[:, lane * LANES : (lane + 1) * LANES]
            totals[span] = totals[span] + column if span in totals else column
        value = jnp.dot(
            terms.astype(jnp.bfloat16), keys[view, :KVL], preferred_element_type=jnp.float32
        )
        if tile > 0:
            value = acc[span % 2] + value
        elif not first:
            value = old_acc[rows] * weights[span] + value
        if tile < parts - 1:
            acc[span % 2] = value
            return
        total = jnp.sum(totals[span], axis=1, keepdims=True)
        if not first:
            total = total + old_total[rows, :1] * weights[span]
        if not last:
            new_acc[rows] = value
            new_top[rows] = jnp.broadcast_to(tops[span], (SPAN, LANES))
            new_total[rows] = jnp.broadcast_to(total, (SPAN, LANES))
            return
        latent_mix = (value / total).astype(jnp.bfloat16)
        for index in range(SPAN // tokens):
            head = span * (SPAN // tokens) + index
            columns = slice(head * VD, (head + 1) * VD)
            out[:, columns] = jnp.dot(
                latent_mix[index * tokens : (index + 1) * tokens],
                up_value[:, columns],
                preferred_element_type=jnp.float32,
            ).astype(out.dtype)

    for span in range(spans + 1):
        for tile in range(parts):
            if span < spans:
                score(span, tile)
            if span > 0:
                mix(span - 1, tile)


def attend(queries, key_at, query_at, sources, state=(), up_value=None):
    rows, parts = queries.shape[0], len(sources)
    tokens = query_at.shape[0]
    if up_value is not None:
        out_shape = jax.ShapeDtypeStruct((tokens, rows // tokens * VD), jnp.bfloat16)
    else:
        out_shape = [
            jax.ShapeDtypeStruct((rows, LANES), jnp.float32),
            jax.ShapeDtypeStruct((rows, LANES), jnp.float32),
            jax.ShapeDtypeStruct((rows, KVL), jnp.float32),
        ]
    operands = [queries, key_at, query_at, *sources, *state]
    specs = [VMEM] * len(operands)
    keys = parts * TILE
    scratch = [
        pltpu.VMEM((keys, WIDE), jnp.bfloat16),
        pltpu.VMEM((2, SPAN, keys), jnp.float32),
        pltpu.VMEM((2, SPAN, KVL), jnp.float32),
    ]
    if up_value is not None:
        operands.append(up_value)
        specs.append(VMEM)
    return kernel_call(
        functools.partial(attend_kernel, parts, not state, up_value is not None),
        out_shape,
        specs,
        scratch,
        2 * rows * keys * (KVL + WIDE),
        keys * WIDE * 4,
    )(*operands)


def chunk_rows(x, y, zl, core):
    ring = jnp.array(OFFSETS, jnp.int32)
    first, second = ring[None, :, None], ring[:, None, None]
    y_at = (y + jnp.where(core == 0, first, second)) % NY
    z_at = (zl + jnp.where(core == 0, second, first)) % NZL
    x_at = jnp.stack(pair_order(x))[None, None, :]
    return (((z_at * NY + y_at) * NC + core) * (NX * CHUNK) + x_at * CHUNK).reshape(-1)


def body(
    hidden_states,
    down_query,
    down_latent,
    query_gain,
    latent_gain,
    up_query,
    up_key,
    up_value,
    owner_table,
):
    tok_rows = hidden_states.shape[0]
    local_heads = up_key.shape[1] // NOPE
    ctx = lax.axis_index("ctx")
    head = lax.axis_index("head")
    x = head % NX
    c, y, zl = ctx % NC, (ctx // NC) % NY, ctx // (NC * NY)
    x_index = x.reshape(1)

    firsts = jnp.concatenate([chunk_rows(x, y, zl, c), chunk_rows(x, y, zl, 1 - c)])
    starts = block_positions(owner_table, firsts, BLK)
    key_at = (starts[:, None] + jnp.arange(CHUNK, dtype=jnp.int32)[None, :]).reshape(1, -1)
    own_rows = ctx * tok_rows + jnp.arange(tok_rows, dtype=jnp.int32)
    own_positions = block_positions(owner_table, own_rows, BLK)
    key_cos, key_sin = (
        jnp.concatenate([table[: CHUNK // 2], table[CHUNK // 2 :]], axis=1)
        for table in rotary_tables(starts[0] + jnp.arange(CHUNK, dtype=jnp.int32))
    )
    query_cos, query_sin = (
        jnp.concatenate([table, table], axis=1) for table in rotary_tables(own_positions)
    )

    key_half = reduce_x(key_down(x_index, hidden_states, down_latent.T))
    key_other = send(key_half, other_half)
    _, hidden_states = lax.optimization_barrier((key_half, hidden_states))
    query_pieces = query_down(x_index, hidden_states, down_query)
    key_pack = kernel_call(
        key_norm_kernel,
        jax.ShapeDtypeStruct((PACK, LANES), jnp.bfloat16),
        [VMEM] * 5,
        [],
        10 * PACK * LANES,
        10 * PACK * LANES,
    )(key_half, key_other, latent_gain.reshape(-1, LANES), key_cos, key_sin)
    key_pack, query_pieces = lax.optimization_barrier((key_pack, query_pieces))
    query_half = reduce_x(query_pieces)
    key_pair = join([key_pack, send(key_pack, pair_x(0))], PACK)
    key_own = join([key_pair, send(key_pair, pair_x(1))], 2 * PACK)
    key_own, query_half = lax.optimization_barrier((key_own, query_half))
    key_first = join(gather_ring(key_own, along_first), key_own.shape[0])

    near = [key_first] + [send(key_first, along_second(-offset)) for offset in OFFSETS[1:3]]

    query_rows = QPACK * CHUNK
    query_latent = kernel_call(
        query_norm_kernel,
        jax.ShapeDtypeStruct(query_half.shape, jnp.bfloat16),
        [VMEM] * 3,
        [],
        10 * query_half.size,
        10 * query_half.size,
    )(query_half, send(query_half, other_half), query_gain.reshape(-1, LANES))
    key_last, query_latent = lax.optimization_barrier((key_first, query_latent))
    near.append(send(key_last, along_second(-OFFSETS[3])))
    query_first = send(query_latent, pair_x(0))
    query_second = send(join([query_latent, query_first], query_rows), pair_x(1))
    queries = kernel_call(
        query_kernel,
        jax.ShapeDtypeStruct((local_heads * tok_rows, WIDE), jnp.bfloat16),
        [SMEM] + [VMEM] * 7,
        [pltpu.VMEM((tok_rows, up_query.shape[0]), jnp.bfloat16)],
        2 * tok_rows * (up_query.size + up_key.size),
        2 * (up_query.size + up_key.size),
        limit=16,
    )(x_index, query_latent, query_first, query_second, up_query, up_key, query_cos, query_sin)

    key_parts = [key_at[:, part * TILE : (part + 1) * TILE] for part in range(2 * len(near))]

    query_at = own_positions.reshape(-1, 1)

    def stage(sources, places, state, last=False):
        return attend(
            queries,
            jnp.concatenate([key_parts[place] for place in places], axis=1),
            query_at,
            sources,
            state,
            up_value if last else None,
        )

    far = [send(part, other_core) for part in near[:3]]
    state = stage(near[:3], [0, 1, 2], ())
    near[3], state = lax.optimization_barrier((near[3], state))
    far.append(send(near[3], other_core))
    state = stage(far[:3], [4, 5, 6], state)
    return stage([near[3], far[3]], [3, 7], state, last=True)


def solution(mesh):
    placed = (
        P("ctx", "head"),
        P("head", None),
        P("head", None),
        P(),
        P(),
        P(None, "head"),
        P(None, "head"),
        P(None, "head"),
        P(),
    )
    return jax.shard_map(
        body, mesh=mesh, in_specs=placed, out_specs=P("ctx", "head"), check_vma=False
    )
```

```python
import functools
import math

import jax
import jax.numpy as jnp
from jax import lax
from jax.experimental import pallas as pl
from jax.experimental.pallas import tpu as pltpu
from jax.sharding import PartitionSpec as P

RD = 64
NOPE = 128
VD = 128
KVL = 512
BLK = 64
LANES = 128
WIDE = KVL + LANES
CHUNK = 32
PACK = CHUNK * (KVL + RD) // LANES
QPACK = 12
TILE = 512
SPAN = 256
NEG = -1e30
SCALE = 1.0 / math.sqrt(NOPE + RD)
LOG2E = math.log2(math.e)
NX, NY, NZ, NZL, NC = 4, 4, 8, 4, 2
AXES = ("ctx", "head")
OFFSETS = (0, -1, 1, 2)
CONTRACT_LAST = (((1,), (1,)), ((), ()))
VMEM = pl.BlockSpec(memory_space=pltpu.VMEM)
SMEM = pl.BlockSpec(memory_space=pltpu.SMEM)
FAR = pl.BlockSpec(memory_space=pltpu.HBM)


def angles(positions):
    half_width = RD // 2
    step_index = jnp.arange(half_width).astype(jnp.float32)
    frequency = jnp.exp(step_index * (-math.log(10000.0) / half_width))
    return positions.astype(jnp.float32)[..., None] * frequency


def rotary_tables(positions):
    table = angles(positions)
    cosines, sines = jnp.cos(table), jnp.sin(table)
    return (
        jnp.concatenate([cosines, cosines], axis=-1),
        jnp.concatenate([-sines, sines], axis=-1),
    )


def block_positions(owner_table, row_index, block_rows):
    slot_index = row_index // block_rows
    block_count = owner_table.shape[0]
    match_table = (owner_table[None, :] == slot_index[:, None]).astype(jnp.int32)
    block_index = jnp.sum(match_table * jnp.arange(block_count, dtype=jnp.int32)[None, :], axis=1)
    return block_index * block_rows + row_index % block_rows


def flat(x, y, z, c):
    ctx = ((z % NZL) * NY + y) * NC + c
    return ctx * (2 * NX) + (z // NZL) * NX + x


def send(value, move):
    pairs = []
    for x in range(NX):
        for y in range(NY):
            for z in range(NZ):
                for c in range(NC):
                    tx, ty, tz, tc = move(x, y, z, c)
                    pairs.append((flat(x, y, z, c), flat(tx % NX, ty % NY, tz % NZ, tc)))
    return lax.ppermute(value, AXES, pairs)


def along_x(step):
    return lambda x, y, z, c: (x + step, y, z, c)


def pair_x(shift):
    return lambda x, y, z, c: (x + (1 if (x + shift) % 2 == 0 else -1), y, z, c)


def pair_order(x):
    partner = (x + NX - 1 + 2 * (x & 1)) & (NX - 1)
    return [x, x + 1 - 2 * (x & 1), partner, partner + 1 - 2 * (partner & 1)]


def step_z(z, step):
    return z - step if abs(step) == 2 and z % 2 else z + step


def along_first(step):
    return lambda x, y, z, c: (x, y + step, z, c) if c == 0 else (x, y, step_z(z, step), c)


def along_second(step):
    return lambda x, y, z, c: (x, y, step_z(z, step), c) if c == 0 else (x, y + step, z, c)


def other_half(x, y, z, c):
    return (x, y, z + NZL, c)


def other_core(x, y, z, c):
    return (x, y, z, 1 - c)


def gather_ring(value, along):
    return [value] + [send(value, along(-offset)) for offset in OFFSETS[1:]]


def kernel_call(kernel, out_shape, in_specs, scratch, flops, moved, limit=32):
    return pl.pallas_call(
        kernel,
        out_shape=out_shape,
        in_specs=in_specs,
        out_specs=jax.tree.map(lambda _: VMEM, out_shape),
        scratch_shapes=scratch,
        compiler_params=pltpu.CompilerParams(vmem_limit_bytes=limit * 2**20),
        cost_estimate=pl.CostEstimate(flops=flops, bytes_accessed=moved, transcendentals=0),
    )


def key_down_kernel(x_ref, hidden_far, weight_far, *refs):
    pieces, (hidden, weight, part, sems) = refs[:NX], refs[NX:]
    half = weight.shape[0] // 2
    loads = [pltpu.make_async_copy(hidden_far, hidden, sems.at[0])]
    for index in range(2):
        rows = pl.ds(index * half, half)
        loads.append(
            pltpu.make_async_copy(weight_far.at[rows], weight.at[rows], sems.at[1 + index])
        )
    for load in loads:
        load.start()
    for load in loads:
        load.wait()
    part[...] = lax.dot_general(
        hidden[...], weight[...], CONTRACT_LAST, preferred_element_type=jnp.float32
    )
    for step, piece in enumerate(pieces):
        start = pl.multiple_of(((x_ref[0] + step) & (NX - 1)) * CHUNK, CHUNK)
        rows = part[pl.ds(start, CHUNK), :]
        for tile in range(KVL // LANES):
            piece[tile * CHUNK : (tile + 1) * CHUNK] = rows[:, tile * LANES : (tile + 1) * LANES]
        rope = rows[:, KVL:]
        piece[KVL // LANES * CHUNK : PACK] = jnp.concatenate(
            [rope[: CHUNK // 2], rope[CHUNK // 2 :]], axis=1
        )


def key_down(x_index, hidden, weight):
    rows = hidden.shape[0]
    return kernel_call(
        key_down_kernel,
        [jax.ShapeDtypeStruct((PACK, LANES), jnp.float32)] * NX,
        [SMEM, FAR, FAR],
        [
            pltpu.VMEM(hidden.shape, hidden.dtype),
            pltpu.VMEM(weight.shape, weight.dtype),
            pltpu.VMEM((rows, weight.shape[0]), jnp.float32),
            pltpu.SemaphoreType.DMA((3,)),
        ],
        2 * rows * weight.size,
        2 * weight.size,
        limit=63,
    )(x_index, hidden, weight)


def query_down_kernel(x_ref, hidden, weight, *refs):
    pieces, part = refs[:NX], refs[NX]
    part[...] = jnp.dot(hidden[...], weight[...], preferred_element_type=jnp.float32)
    for step, piece in enumerate(pieces):
        start = pl.multiple_of(((x_ref[0] + step) & (NX - 1)) * CHUNK, CHUNK)
        for tile in range(QPACK):
            piece[tile * CHUNK : (tile + 1) * CHUNK] = part[
                pl.ds(start, CHUNK), tile * LANES : (tile + 1) * LANES
            ]


def query_down(x_index, hidden, weight):
    rows = hidden.shape[0]
    return kernel_call(
        query_down_kernel,
        [jax.ShapeDtypeStruct((QPACK * CHUNK, LANES), jnp.float32)] * NX,
        [SMEM, VMEM, VMEM],
        [pltpu.VMEM((rows, weight.shape[1]), jnp.float32)],
        2 * rows * weight.size,
        2 * weight.size,
        limit=16,
    )(x_index, hidden, weight)


def sum_kernel(own, one, two, three, out):
    out[...] = own[...] + one[...] + two[...] + three[...]


def reduce_x(pieces):
    arrived = [send(pieces[step], along_x(step)) for step in (1, 2, 3)]
    return kernel_call(
        sum_kernel,
        jax.ShapeDtypeStruct(pieces[0].shape, jnp.float32),
        [VMEM] * 4,
        [],
        4 * pieces[0].size,
        16 * pieces[0].size,
    )(pieces[0], *arrived)


def join_kernel(rows, *refs):
    pieces, out = refs[:-1], refs[-1]
    for index, piece in enumerate(pieces):
        out[index * rows : (index + 1) * rows] = piece[:rows]


def join(pieces, rows):
    shape = (len(pieces) * rows, LANES)
    size = len(pieces) * rows * LANES
    return kernel_call(
        functools.partial(join_kernel, rows),
        jax.ShapeDtypeStruct(shape, pieces[0].dtype),
        [VMEM] * len(pieces),
        [],
        size,
        4 * size,
    )(*pieces)


def load_kernel(count, *refs):
    sources, outs, sems = refs[:count], refs[count : 2 * count], refs[2 * count]
    loads = []
    for source, out in zip(sources, outs):
        rows = source.shape[0] // 2
        for half in range(2):
            view = pl.ds(half * rows, rows)
            loads.append(
                pltpu.make_async_copy(source.at[view], out.at[view], sems.at[len(loads)])
            )
    for load in loads:
        load.start()
    for load in loads:
        load.wait()


def load_weights(*weights):
    return kernel_call(
        functools.partial(load_kernel, len(weights)),
        [jax.ShapeDtypeStruct(weight.shape, weight.dtype) for weight in weights],
        [FAR] * len(weights),
        [pltpu.SemaphoreType.DMA((2 * len(weights),))],
        0,
        4 * sum(weight.size for weight in weights),
    )(*weights)


def exchange_halves(values, lanes):
    half = RD // 2
    left = pltpu.roll(values, LANES - half, 1)
    right = pltpu.roll(values, half, 1)
    return jnp.where((lanes & half) == 0, left, right)


def norm_tiles(total, gain, out, start, count):
    tiles = [total[start + i * CHUNK : start + (i + 1) * CHUNK] for i in range(count)]
    squares = sum(tile * tile for tile in tiles)
    mean = jnp.sum(squares, axis=1, keepdims=True) * (1.0 / (count * LANES))
    factor = lax.rsqrt(mean + 1e-06)
    for index, tile in enumerate(tiles):
        out[start + index * CHUNK : start + (index + 1) * CHUNK] = (
            tile * factor * gain[index : index + 1, :]
        ).astype(out.dtype)


def key_norm_kernel(own, other, gain, cosines, sines, out):
    total = own[...] + other[...]
    norm_tiles(total, gain, out, 0, KVL // LANES)
    rope = total[KVL // LANES * CHUNK :]
    lanes = lax.broadcasted_iota(jnp.int32, rope.shape, 1)
    out[KVL // LANES * CHUNK :] = (
        rope * cosines[...] + exchange_halves(rope, lanes) * sines[...]
    ).astype(out.dtype)


def query_norm_kernel(own, other, gain, out):
    norm_tiles(own[...] + other[...], gain, out, 0, QPACK)


def query_kernel(x_ref, own, first, second, up_query, up_key, cosines, sines, out, rows):
    pair = 2 * (NOPE + RD)
    pairs = up_query.shape[1] // pair
    size = QPACK * CHUNK
    places = zip(pair_order(x_ref[0]), (own, first, second, second), (0, 0, 0, size))
    for place, piece, at in places:
        start = pl.multiple_of(place * CHUNK, CHUNK)
        for tile in range(QPACK):
            rows[pl.ds(start, CHUNK), tile * LANES : (tile + 1) * LANES] = piece[
                at + tile * CHUNK : at + (tile + 1) * CHUNK
            ]
    tokens = rows.shape[0]
    lanes = lax.broadcasted_iota(jnp.int32, (tokens, LANES), 1)
    for index in range(pairs):
        full = jnp.dot(
            rows[...],
            up_query[:, index * pair : (index + 1) * pair],
            preferred_element_type=jnp.float32,
        )
        first, second, third = (full[:, i * LANES : (i + 1) * LANES] for i in range(3))
        second_half, third_half = pltpu.roll(second, RD, 1), pltpu.roll(third, RD, 1)
        heads = (
            (first, second),
            (jnp.where(lanes < RD, second_half, third_half), third_half),
        )
        for offset, (nope, rope) in enumerate(heads):
            head = 2 * index + offset
            absorbed = lax.dot_general(
                nope.astype(jnp.bfloat16),
                up_key[:, head * NOPE : (head + 1) * NOPE],
                CONTRACT_LAST,
                preferred_element_type=jnp.float32,
            )
            out[head * tokens : (head + 1) * tokens, :KVL] = absorbed.astype(out.dtype)
            turned = rope * cosines[...] + exchange_halves(rope, lanes) * sines[...]
            out[head * tokens : (head + 1) * tokens, KVL:] = jnp.where(
                lanes < RD, turned, 0.0
            ).astype(out.dtype)


def attend_kernel(parts, first, last, *refs):
    refs = list(refs)
    queries, key_at, query_at = refs[:3]
    sources, refs = refs[3 : 3 + parts], refs[3 + parts :]
    if not first:
        (old_top, old_total, old_acc), refs = refs[:3], refs[3:]
    if last:
        up_value, out, refs = refs[0], refs[1], refs[2:]
    else:
        (new_top, new_total, new_acc), refs = refs[:3], refs[3:]
    keys, scores, acc = refs

    chunks = TILE // CHUNK
    for part, source in enumerate(sources):
        for chunk in range(chunks):
            to, at = part * TILE + chunk * CHUNK, chunk * PACK
            for tile in range(KVL // LANES):
                keys[to : to + CHUNK, tile * LANES : (tile + 1) * LANES] = source[
                    at + tile * CHUNK : at + (tile + 1) * CHUNK
                ]
            rope = source[at + KVL // LANES * CHUNK : at + PACK]
            keys[to : to + CHUNK // 2, KVL:] = rope
            keys[to + CHUNK // 2 : to + CHUNK, KVL:] = jnp.concatenate(
                [rope[:, RD:], rope[:, :RD]], axis=1
            )

    tokens = query_at.shape[0]
    rows_at = jnp.concatenate([query_at[...]] * (SPAN // tokens), axis=0)
    spans = queries.shape[0] // SPAN
    tops, totals, weights = {}, {}, {}

    def score(span, tile):
        view = slice(tile * TILE, (tile + 1) * TILE)
        value = lax.dot_general(
            queries[span * SPAN : (span + 1) * SPAN],
            keys[view],
            CONTRACT_LAST,
            preferred_element_type=jnp.float32,
        )
        value = jnp.where(key_at[:, view] <= rows_at, value, NEG)
        scores[span % 2, :, view] = value
        for lane in range(TILE // LANES):
            column = value[:, lane * LANES : (lane + 1) * LANES]
            tops[span] = jnp.maximum(tops[span], column) if span in tops else column

    def mix(span, tile):
        rows = slice(span * SPAN, (span + 1) * SPAN)
        view = slice(tile * TILE, (tile + 1) * TILE)
        if tile == 0:
            top = jnp.max(tops[span], axis=1, keepdims=True)
            if not first:
                before = old_top[rows, :1]
                top = jnp.maximum(top, before)
                weights[span] = jnp.exp2((before - top) * (SCALE * LOG2E))
            tops[span] = top
        terms = jnp.exp2((scores[span % 2, :, view] - tops[span]) * (SCALE * LOG2E))
        for lane in range(TILE // LANES):
            column = terms[:, lane * LANES : (lane + 1) * LANES]
            totals[span] = totals[span] + column if span in totals else column
        value = jnp.dot(
            terms.astype(jnp.bfloat16), keys[view, :KVL], preferred_element_type=jnp.float32
        )
        if tile > 0:
            value = acc[span % 2] + value
        elif not first:
            value = old_acc[rows] * weights[span] + value
        if tile < parts - 1:
            acc[span % 2] = value
            return
        total = jnp.sum(totals[span], axis=1, keepdims=True)
        if not first:
            total = total + old_total[rows, :1] * weights[span]
        if not last:
            new_acc[rows] = value
            new_top[rows] = jnp.broadcast_to(tops[span], (SPAN, LANES))
            new_total[rows] = jnp.broadcast_to(total, (SPAN, LANES))
            return
        latent_mix = (value / total).astype(jnp.bfloat16)
        for index in range(SPAN // tokens):
            head = span * (SPAN // tokens) + index
            columns = slice(head * VD, (head + 1) * VD)
            out[:, columns] = jnp.dot(
                latent_mix[index * tokens : (index + 1) * tokens],
                up_value[:, columns],
                preferred_element_type=jnp.float32,
            ).astype(out.dtype)

    for span in range(spans + 1):
        for tile in range(parts):
            if span < spans:
                score(span, tile)
            if span > 0:
                mix(span - 1, tile)


def attend(queries, key_at, query_at, sources, state=(), up_value=None):
    rows, parts = queries.shape[0], len(sources)
    tokens = query_at.shape[0]
    if up_value is not None:
        out_shape = jax.ShapeDtypeStruct((tokens, rows // tokens * VD), jnp.bfloat16)
    else:
        out_shape = [
            jax.ShapeDtypeStruct((rows, LANES), jnp.float32),
            jax.ShapeDtypeStruct((rows, LANES), jnp.float32),
            jax.ShapeDtypeStruct((rows, KVL), jnp.float32),
        ]
    operands = [queries, key_at, query_at, *sources, *state]
    specs = [VMEM] * len(operands)
    keys = parts * TILE
    scratch = [
        pltpu.VMEM((keys, WIDE), jnp.bfloat16),
        pltpu.VMEM((2, SPAN, keys), jnp.float32),
        pltpu.VMEM((2, SPAN, KVL), jnp.float32),
    ]
    if up_value is not None:
        operands.append(up_value)
        specs.append(VMEM)
    return kernel_call(
        functools.partial(attend_kernel, parts, not state, up_value is not None),
        out_shape,
        specs,
        scratch,
        2 * rows * keys * (KVL + WIDE),
        keys * WIDE * 4,
    )(*operands)


def chunk_rows(x, y, zl, core):
    ring = jnp.array(OFFSETS, jnp.int32)
    first, second = ring[None, :, None], ring[:, None, None]
    y_at = (y + jnp.where(core == 0, first, second)) % NY
    z_at = (zl + jnp.where(core == 0, second, first)) % NZL
    x_at = jnp.stack(pair_order(x))[None, None, :]
    return (((z_at * NY + y_at) * NC + core) * (NX * CHUNK) + x_at * CHUNK).reshape(-1)


def body(
    hidden_states,
    down_query,
    down_latent,
    query_gain,
    latent_gain,
    up_query,
    up_key,
    up_value,
    owner_table,
):
    tok_rows = hidden_states.shape[0]
    local_heads = up_key.shape[1] // NOPE
    ctx = lax.axis_index("ctx")
    head = lax.axis_index("head")
    x = head % NX
    c, y, zl = ctx % NC, (ctx // NC) % NY, ctx // (NC * NY)
    x_index = x.reshape(1)

    firsts = jnp.concatenate([chunk_rows(x, y, zl, c), chunk_rows(x, y, zl, 1 - c)])
    starts = block_positions(owner_table, firsts, BLK)
    key_at = (starts[:, None] + jnp.arange(CHUNK, dtype=jnp.int32)[None, :]).reshape(1, -1)
    own_rows = ctx * tok_rows + jnp.arange(tok_rows, dtype=jnp.int32)
    own_positions = block_positions(owner_table, own_rows, BLK)
    key_cos, key_sin = (
        jnp.concatenate([table[: CHUNK // 2], table[CHUNK // 2 :]], axis=1)
        for table in rotary_tables(starts[0] + jnp.arange(CHUNK, dtype=jnp.int32))
    )
    query_cos, query_sin = (
        jnp.concatenate([table, table], axis=1) for table in rotary_tables(own_positions)
    )

    key_half = reduce_x(key_down(x_index, hidden_states, down_latent.T))
    key_other = send(key_half, other_half)
    _, hidden_states = lax.optimization_barrier((key_half, hidden_states))
    query_pieces = query_down(x_index, hidden_states, down_query)
    key_pack = kernel_call(
        key_norm_kernel,
        jax.ShapeDtypeStruct((PACK, LANES), jnp.bfloat16),
        [VMEM] * 5,
        [],
        10 * PACK * LANES,
        10 * PACK * LANES,
    )(key_half, key_other, latent_gain.reshape(-1, LANES), key_cos, key_sin)
    key_pack, query_pieces = lax.optimization_barrier((key_pack, query_pieces))
    query_half = reduce_x(query_pieces)
    key_pair = join([key_pack, send(key_pack, pair_x(0))], PACK)
    key_own = join([key_pair, send(key_pair, pair_x(1))], 2 * PACK)
    key_own, query_half = lax.optimization_barrier((key_own, query_half))
    key_first = join(gather_ring(key_own, along_first), key_own.shape[0])

    near = [key_first] + [send(key_first, along_second(-offset)) for offset in OFFSETS[1:3]]

    query_rows = QPACK * CHUNK
    query_latent = kernel_call(
        query_norm_kernel,
        jax.ShapeDtypeStruct(query_half.shape, jnp.bfloat16),
        [VMEM] * 3,
        [],
        10 * query_half.size,
        10 * query_half.size,
    )(query_half, send(query_half, other_half), query_gain.reshape(-1, LANES))
    key_last, query_latent = lax.optimization_barrier((key_first, query_latent))
    near.append(send(key_last, along_second(-OFFSETS[3])))
    query_first = send(query_latent, pair_x(0))
    query_first, up_query, up_key = lax.optimization_barrier((query_first, up_query, up_key))
    query_second = send(join([query_latent, query_first], query_rows), pair_x(1))
    query_second, (up_query, up_key) = lax.optimization_barrier(
        (query_second, load_weights(up_query, up_key))
    )
    queries = kernel_call(
        query_kernel,
        jax.ShapeDtypeStruct((local_heads * tok_rows, WIDE), jnp.bfloat16),
        [SMEM] + [VMEM] * 7,
        [pltpu.VMEM((tok_rows, up_query.shape[0]), jnp.bfloat16)],
        2 * tok_rows * (up_query.size + up_key.size),
        2 * (up_query.size + up_key.size),
        limit=16,
    )(x_index, query_latent, query_first, query_second, up_query, up_key, query_cos, query_sin)

    key_parts = [key_at[:, part * TILE : (part + 1) * TILE] for part in range(2 * len(near))]

    query_at = own_positions.reshape(-1, 1)

    def stage(sources, places, state, last=False):
        return attend(
            queries,
            jnp.concatenate([key_parts[place] for place in places], axis=1),
            query_at,
            sources,
            state,
            up_value if last else None,
        )

    far = [send(part, other_core) for part in near[:3]]
    state = stage(near[:3], [0, 1, 2], ())
    near[3], state = lax.optimization_barrier((near[3], state))
    far.append(send(near[3], other_core))
    state = stage(far[:3], [4, 5, 6], state)
    return stage([near[3], far[3]], [3, 7], state, last=True)


def solution(mesh):
    placed = (
        P("ctx", "head"),
        P("head", None),
        P("head", None),
        P(),
        P(),
        P(None, "head"),
        P(None, "head"),
        P(None, "head"),
        P(),
    )
    return jax.shard_map(
        body, mesh=mesh, in_specs=placed, out_specs=P("ctx", "head"), check_vma=False
    )
```

```python
import functools
import math

import jax
import jax.numpy as jnp
from jax import lax
from jax.experimental import pallas as pl
from jax.experimental.pallas import tpu as pltpu
from jax.sharding import PartitionSpec as P

RD = 64
NOPE = 128
VD = 128
KVL = 512
BLK = 64
LANES = 128
WIDE = KVL + LANES
CHUNK = 32
PACK = CHUNK * (KVL + RD) // LANES
QPACK = 12
TILE = 512
SPAN = 256
NEG = -1e30
SCALE = 1.0 / math.sqrt(NOPE + RD)
LOG2E = math.log2(math.e)
NX, NY, NZ, NZL, NC = 4, 4, 8, 4, 2
AXES = ("ctx", "head")
OFFSETS = (0, -1, 1, 2)
CONTRACT_LAST = (((1,), (1,)), ((), ()))
VMEM = pl.BlockSpec(memory_space=pltpu.VMEM)
SMEM = pl.BlockSpec(memory_space=pltpu.SMEM)
FAR = pl.BlockSpec(memory_space=pltpu.HBM)


def angles(positions):
    half_width = RD // 2
    step_index = jnp.arange(half_width).astype(jnp.float32)
    frequency = jnp.exp(step_index * (-math.log(10000.0) / half_width))
    return positions.astype(jnp.float32)[..., None] * frequency


def rotary_tables(positions):
    table = angles(positions)
    cosines, sines = jnp.cos(table), jnp.sin(table)
    return (
        jnp.concatenate([cosines, cosines], axis=-1),
        jnp.concatenate([-sines, sines], axis=-1),
    )


def block_positions(owner_table, row_index, block_rows):
    slot_index = row_index // block_rows
    block_count = owner_table.shape[0]
    match_table = (owner_table[None, :] == slot_index[:, None]).astype(jnp.int32)
    block_index = jnp.sum(match_table * jnp.arange(block_count, dtype=jnp.int32)[None, :], axis=1)
    return block_index * block_rows + row_index % block_rows


def flat(x, y, z, c):
    ctx = ((z % NZL) * NY + y) * NC + c
    return ctx * (2 * NX) + (z // NZL) * NX + x


def send(value, move):
    pairs = []
    for x in range(NX):
        for y in range(NY):
            for z in range(NZ):
                for c in range(NC):
                    tx, ty, tz, tc = move(x, y, z, c)
                    pairs.append((flat(x, y, z, c), flat(tx % NX, ty % NY, tz % NZ, tc)))
    return lax.ppermute(value, AXES, pairs)


def along_x(step):
    return lambda x, y, z, c: (x + step, y, z, c)


def pair_x(shift):
    return lambda x, y, z, c: (x + (1 if (x + shift) % 2 == 0 else -1), y, z, c)


def pair_order(x):
    partner = (x + NX - 1 + 2 * (x & 1)) & (NX - 1)
    return [x, x + 1 - 2 * (x & 1), partner, partner + 1 - 2 * (partner & 1)]


def step_z(z, step):
    return z - step if abs(step) == 2 and z % 2 else z + step


def along_first(step):
    return lambda x, y, z, c: (x, y + step, z, c) if c == 0 else (x, y, step_z(z, step), c)


def along_second(step):
    return lambda x, y, z, c: (x, y, step_z(z, step), c) if c == 0 else (x, y + step, z, c)


def other_half(x, y, z, c):
    return (x, y, z + NZL, c)


def other_core(x, y, z, c):
    return (x, y, z, 1 - c)


def gather_ring(value, along):
    return [value] + [send(value, along(-offset)) for offset in OFFSETS[1:]]


def kernel_call(kernel, out_shape, in_specs, scratch, flops, moved, limit=32):
    return pl.pallas_call(
        kernel,
        out_shape=out_shape,
        in_specs=in_specs,
        out_specs=jax.tree.map(lambda _: VMEM, out_shape),
        scratch_shapes=scratch,
        compiler_params=pltpu.CompilerParams(vmem_limit_bytes=limit * 2**20),
        cost_estimate=pl.CostEstimate(flops=flops, bytes_accessed=moved, transcendentals=0),
    )


def key_down_kernel(x_ref, hidden_far, weight_far, *refs):
    pieces, (hidden, weight, part, sems) = refs[:NX], refs[NX:]
    half = weight.shape[0] // 2
    loads = [pltpu.make_async_copy(hidden_far, hidden, sems.at[0])]
    for index in range(2):
        rows = pl.ds(index * half, half)
        loads.append(
            pltpu.make_async_copy(weight_far.at[rows], weight.at[rows], sems.at[1 + index])
        )
    for load in loads:
        load.start()
    for load in loads:
        load.wait()
    part[...] = lax.dot_general(
        hidden[...], weight[...], CONTRACT_LAST, preferred_element_type=jnp.float32
    )
    for step, piece in enumerate(pieces):
        start = pl.multiple_of(((x_ref[0] + step) & (NX - 1)) * CHUNK, CHUNK)
        rows = part[pl.ds(start, CHUNK), :]
        for tile in range(KVL // LANES):
            piece[tile * CHUNK : (tile + 1) * CHUNK] = rows[:, tile * LANES : (tile + 1) * LANES]
        rope = rows[:, KVL:]
        piece[KVL // LANES * CHUNK : PACK] = jnp.concatenate(
            [rope[: CHUNK // 2], rope[CHUNK // 2 :]], axis=1
        )


def key_down(x_index, hidden, weight):
    rows = hidden.shape[0]
    return kernel_call(
        key_down_kernel,
        [jax.ShapeDtypeStruct((PACK, LANES), jnp.float32)] * NX,
        [SMEM, FAR, FAR],
        [
            pltpu.VMEM(hidden.shape, hidden.dtype),
            pltpu.VMEM(weight.shape, weight.dtype),
            pltpu.VMEM((rows, weight.shape[0]), jnp.float32),
            pltpu.SemaphoreType.DMA((3,)),
        ],
        2 * rows * weight.size,
        2 * weight.size,
        limit=63,
    )(x_index, hidden, weight)


def query_down_kernel(x_ref, hidden, weight, *refs):
    pieces, part = refs[:NX], refs[NX]
    part[...] = jnp.dot(hidden[...], weight[...], preferred_element_type=jnp.float32)
    for step, piece in enumerate(pieces):
        start = pl.multiple_of(((x_ref[0] + step) & (NX - 1)) * CHUNK, CHUNK)
        for tile in range(QPACK):
            piece[tile * CHUNK : (tile + 1) * CHUNK] = part[
                pl.ds(start, CHUNK), tile * LANES : (tile + 1) * LANES
            ]


def query_down(x_index, hidden, weight):
    rows = hidden.shape[0]
    return kernel_call(
        query_down_kernel,
        [jax.ShapeDtypeStruct((QPACK * CHUNK, LANES), jnp.float32)] * NX,
        [SMEM, VMEM, VMEM],
        [pltpu.VMEM((rows, weight.shape[1]), jnp.float32)],
        2 * rows * weight.size,
        2 * weight.size,
        limit=16,
    )(x_index, hidden, weight)


def sum_kernel(own, one, two, three, out):
    out[...] = own[...] + one[...] + two[...] + three[...]


def reduce_x(pieces):
    arrived = [send(pieces[step], along_x(step)) for step in (1, 2, 3)]
    return kernel_call(
        sum_kernel,
        jax.ShapeDtypeStruct(pieces[0].shape, jnp.float32),
        [VMEM] * 4,
        [],
        4 * pieces[0].size,
        16 * pieces[0].size,
    )(pieces[0], *arrived)


def join_kernel(rows, *refs):
    pieces, out = refs[:-1], refs[-1]
    for index, piece in enumerate(pieces):
        out[index * rows : (index + 1) * rows] = piece[:rows]


def join(pieces, rows):
    shape = (len(pieces) * rows, LANES)
    size = len(pieces) * rows * LANES
    return kernel_call(
        functools.partial(join_kernel, rows),
        jax.ShapeDtypeStruct(shape, pieces[0].dtype),
        [VMEM] * len(pieces),
        [],
        size,
        4 * size,
    )(*pieces)


def load_kernel(count, *refs):
    sources, outs, sems = refs[:count], refs[count : 2 * count], refs[2 * count]
    loads = []
    for source, out in zip(sources, outs):
        rows = source.shape[0] // 2
        for half in range(2):
            view = pl.ds(half * rows, rows)
            loads.append(
                pltpu.make_async_copy(source.at[view], out.at[view], sems.at[len(loads)])
            )
    for load in loads:
        load.start()
    for load in loads:
        load.wait()


def load_weights(*weights):
    return kernel_call(
        functools.partial(load_kernel, len(weights)),
        [jax.ShapeDtypeStruct(weight.shape, weight.dtype) for weight in weights],
        [FAR] * len(weights),
        [pltpu.SemaphoreType.DMA((2 * len(weights),))],
        0,
        4 * sum(weight.size for weight in weights),
    )(*weights)


def exchange_halves(values, lanes):
    half = RD // 2
    left = pltpu.roll(values, LANES - half, 1)
    right = pltpu.roll(values, half, 1)
    return jnp.where((lanes & half) == 0, left, right)


def norm_tiles(total, gain, out, start, count):
    tiles = [total[start + i * CHUNK : start + (i + 1) * CHUNK] for i in range(count)]
    squares = sum(tile * tile for tile in tiles)
    mean = jnp.sum(squares, axis=1, keepdims=True) * (1.0 / (count * LANES))
    factor = lax.rsqrt(mean + 1e-06)
    for index, tile in enumerate(tiles):
        out[start + index * CHUNK : start + (index + 1) * CHUNK] = (
            tile * factor * gain[index : index + 1, :]
        ).astype(out.dtype)


def key_norm_kernel(own, other, gain, cosines, sines, out):
    total = own[...] + other[...]
    norm_tiles(total, gain, out, 0, KVL // LANES)
    rope = total[KVL // LANES * CHUNK :]
    lanes = lax.broadcasted_iota(jnp.int32, rope.shape, 1)
    out[KVL // LANES * CHUNK :] = (
        rope * cosines[...] + exchange_halves(rope, lanes) * sines[...]
    ).astype(out.dtype)


def query_norm_kernel(own, other, gain, out):
    norm_tiles(own[...] + other[...], gain, out, 0, QPACK)


def query_kernel(x_ref, own, first, second, up_query, up_key, cosines, sines, out, rows):
    pair = 2 * (NOPE + RD)
    pairs = up_query.shape[1] // pair
    size = QPACK * CHUNK
    places = zip(pair_order(x_ref[0]), (own, first, second, second), (0, 0, 0, size))
    for place, piece, at in places:
        start = pl.multiple_of(place * CHUNK, CHUNK)
        for tile in range(QPACK):
            rows[pl.ds(start, CHUNK), tile * LANES : (tile + 1) * LANES] = piece[
                at + tile * CHUNK : at + (tile + 1) * CHUNK
            ]
    tokens = rows.shape[0]
    lanes = lax.broadcasted_iota(jnp.int32, (tokens, LANES), 1)
    for index in range(pairs):
        full = jnp.dot(
            rows[...],
            up_query[:, index * pair : (index + 1) * pair],
            preferred_element_type=jnp.float32,
        )
        first, second, third = (full[:, i * LANES : (i + 1) * LANES] for i in range(3))
        second_half, third_half = pltpu.roll(second, RD, 1), pltpu.roll(third, RD, 1)
        heads = (
            (first, second),
            (jnp.where(lanes < RD, second_half, third_half), third_half),
        )
        for offset, (nope, rope) in enumerate(heads):
            head = 2 * index + offset
            absorbed = lax.dot_general(
                nope.astype(jnp.bfloat16),
                up_key[:, head * NOPE : (head + 1) * NOPE],
                CONTRACT_LAST,
                preferred_element_type=jnp.float32,
            )
            out[head * tokens : (head + 1) * tokens, :KVL] = absorbed.astype(out.dtype)
            turned = rope * cosines[...] + exchange_halves(rope, lanes) * sines[...]
            out[head * tokens : (head + 1) * tokens, KVL:] = jnp.where(
                lanes < RD, turned, 0.0
            ).astype(out.dtype)


def attend_kernel(parts, first, last, *refs):
    refs = list(refs)
    queries, key_at, query_at = refs[:3]
    sources, refs = refs[3 : 3 + parts], refs[3 + parts :]
    if not first:
        (old_top, old_total, old_acc), refs = refs[:3], refs[3:]
    if last:
        up_value, out, refs = refs[0], refs[1], refs[2:]
    else:
        (new_top, new_total, new_acc), refs = refs[:3], refs[3:]
    keys, scores, acc = refs

    chunks = TILE // CHUNK
    for part, source in enumerate(sources):
        for chunk in range(chunks):
            to, at = part * TILE + chunk * CHUNK, chunk * PACK
            for tile in range(KVL // LANES):
                keys[to : to + CHUNK, tile * LANES : (tile + 1) * LANES] = source[
                    at + tile * CHUNK : at + (tile + 1) * CHUNK
                ]
            rope = source[at + KVL // LANES * CHUNK : at + PACK]
            keys[to : to + CHUNK // 2, KVL:] = rope
            keys[to + CHUNK // 2 : to + CHUNK, KVL:] = jnp.concatenate(
                [rope[:, RD:], rope[:, :RD]], axis=1
            )

    tokens = query_at.shape[0]
    rows_at = jnp.concatenate([query_at[...]] * (SPAN // tokens), axis=0)
    spans = queries.shape[0] // SPAN
    tops, totals, weights = {}, {}, {}

    def score(span, tile):
        view = slice(tile * TILE, (tile + 1) * TILE)
        value = lax.dot_general(
            queries[span * SPAN : (span + 1) * SPAN],
            keys[view],
            CONTRACT_LAST,
            preferred_element_type=jnp.float32,
        )
        value = jnp.where(key_at[:, view] <= rows_at, value, NEG)
        scores[span % 2, :, view] = value
        for lane in range(TILE // LANES):
            column = value[:, lane * LANES : (lane + 1) * LANES]
            tops[span] = jnp.maximum(tops[span], column) if span in tops else column

    def mix(span, tile):
        rows = slice(span * SPAN, (span + 1) * SPAN)
        view = slice(tile * TILE, (tile + 1) * TILE)
        if tile == 0:
            top = jnp.max(tops[span], axis=1, keepdims=True)
            if not first:
                before = old_top[rows, :1]
                top = jnp.maximum(top, before)
                weights[span] = jnp.exp2((before - top) * (SCALE * LOG2E))
            tops[span] = top
        terms = jnp.exp2((scores[span % 2, :, view] - tops[span]) * (SCALE * LOG2E))
        for lane in range(TILE // LANES):
            column = terms[:, lane * LANES : (lane + 1) * LANES]
            totals[span] = totals[span] + column if span in totals else column
        value = jnp.dot(
            terms.astype(jnp.bfloat16), keys[view, :KVL], preferred_element_type=jnp.float32
        )
        if tile > 0:
            value = acc[span % 2] + value
        elif not first:
            value = old_acc[rows] * weights[span] + value
        if tile < parts - 1:
            acc[span % 2] = value
            return
        total = jnp.sum(totals[span], axis=1, keepdims=True)
        if not first:
            total = total + old_total[rows, :1] * weights[span]
        if not last:
            new_acc[rows] = value
            new_top[rows] = jnp.broadcast_to(tops[span], (SPAN, LANES))
            new_total[rows] = jnp.broadcast_to(total, (SPAN, LANES))
            return
        latent_mix = (value / total).astype(jnp.bfloat16)
        for index in range(SPAN // tokens):
            head = span * (SPAN // tokens) + index
            columns = slice(head * VD, (head + 1) * VD)
            out[:, columns] = jnp.dot(
                latent_mix[index * tokens : (index + 1) * tokens],
                up_value[:, columns],
                preferred_element_type=jnp.float32,
            ).astype(out.dtype)

    for span in range(spans + 1):
        for tile in range(parts):
            if span < spans:
                score(span, tile)
            if span > 0:
                mix(span - 1, tile)


def attend(queries, key_at, query_at, sources, state=(), up_value=None):
    rows, parts = queries.shape[0], len(sources)
    tokens = query_at.shape[0]
    if up_value is not None:
        out_shape = jax.ShapeDtypeStruct((tokens, rows // tokens * VD), jnp.bfloat16)
    else:
        out_shape = [
            jax.ShapeDtypeStruct((rows, LANES), jnp.float32),
            jax.ShapeDtypeStruct((rows, LANES), jnp.float32),
            jax.ShapeDtypeStruct((rows, KVL), jnp.float32),
        ]
    operands = [queries, key_at, query_at, *sources, *state]
    specs = [VMEM] * len(operands)
    keys = parts * TILE
    scratch = [
        pltpu.VMEM((keys, WIDE), jnp.bfloat16),
        pltpu.VMEM((2, SPAN, keys), jnp.float32),
        pltpu.VMEM((2, SPAN, KVL), jnp.float32),
    ]
    if up_value is not None:
        operands.append(up_value)
        specs.append(VMEM)
    return kernel_call(
        functools.partial(attend_kernel, parts, not state, up_value is not None),
        out_shape,
        specs,
        scratch,
        2 * rows * keys * (KVL + WIDE),
        keys * WIDE * 4,
    )(*operands)


def chunk_rows(x, y, zl, core):
    ring = jnp.array(OFFSETS, jnp.int32)
    first, second = ring[None, :, None], ring[:, None, None]
    y_at = (y + jnp.where(core == 0, first, second)) % NY
    z_at = (zl + jnp.where(core == 0, second, first)) % NZL
    x_at = jnp.stack(pair_order(x))[None, None, :]
    return (((z_at * NY + y_at) * NC + core) * (NX * CHUNK) + x_at * CHUNK).reshape(-1)


def body(
    hidden_states,
    down_query,
    down_latent,
    query_gain,
    latent_gain,
    up_query,
    up_key,
    up_value,
    owner_table,
):
    tok_rows = hidden_states.shape[0]
    local_heads = up_key.shape[1] // NOPE
    ctx = lax.axis_index("ctx")
    head = lax.axis_index("head")
    x = head % NX
    c, y, zl = ctx % NC, (ctx // NC) % NY, ctx // (NC * NY)
    x_index = x.reshape(1)

    firsts = jnp.concatenate([chunk_rows(x, y, zl, c), chunk_rows(x, y, zl, 1 - c)])
    starts = block_positions(owner_table, firsts, BLK)
    key_at = (starts[:, None] + jnp.arange(CHUNK, dtype=jnp.int32)[None, :]).reshape(1, -1)
    own_rows = ctx * tok_rows + jnp.arange(tok_rows, dtype=jnp.int32)
    own_positions = block_positions(owner_table, own_rows, BLK)
    key_cos, key_sin = (
        jnp.concatenate([table[: CHUNK // 2], table[CHUNK // 2 :]], axis=1)
        for table in rotary_tables(starts[0] + jnp.arange(CHUNK, dtype=jnp.int32))
    )
    query_cos, query_sin = (
        jnp.concatenate([table, table], axis=1) for table in rotary_tables(own_positions)
    )

    key_half = reduce_x(key_down(x_index, hidden_states, down_latent.T))
    key_other = send(key_half, other_half)
    _, hidden_states = lax.optimization_barrier((key_half, hidden_states))
    query_pieces = query_down(x_index, hidden_states, down_query)
    key_pack = kernel_call(
        key_norm_kernel,
        jax.ShapeDtypeStruct((PACK, LANES), jnp.bfloat16),
        [VMEM] * 5,
        [],
        10 * PACK * LANES,
        10 * PACK * LANES,
    )(key_half, key_other, latent_gain.reshape(-1, LANES), key_cos, key_sin)
    key_pack, query_pieces = lax.optimization_barrier((key_pack, query_pieces))
    query_half = reduce_x(query_pieces)
    key_pair = join([key_pack, send(key_pack, pair_x(0))], PACK)
    key_own = join([key_pair, send(key_pair, pair_x(1))], 2 * PACK)
    key_own, query_half = lax.optimization_barrier((key_own, query_half))
    key_first = join(gather_ring(key_own, along_first), key_own.shape[0])

    near = [key_first] + [send(key_first, along_second(-offset)) for offset in OFFSETS[1:3]]

    query_rows = QPACK * CHUNK
    query_latent = kernel_call(
        query_norm_kernel,
        jax.ShapeDtypeStruct(query_half.shape, jnp.bfloat16),
        [VMEM] * 3,
        [],
        10 * query_half.size,
        10 * query_half.size,
    )(query_half, send(query_half, other_half), query_gain.reshape(-1, LANES))
    query_first = send(query_latent, pair_x(0))
    query_first, up_query, up_key = lax.optimization_barrier((query_first, up_query, up_key))
    query_pair = join([query_latent, query_first], query_rows)
    key_last, query_pair = lax.optimization_barrier((key_first, query_pair))
    query_second = send(query_pair, pair_x(1))
    near.append(send(key_last, along_second(-OFFSETS[3])))
    query_second, (up_query, up_key) = lax.optimization_barrier(
        (query_second, load_weights(up_query, up_key))
    )
    queries = kernel_call(
        query_kernel,
        jax.ShapeDtypeStruct((local_heads * tok_rows, WIDE), jnp.bfloat16),
        [SMEM] + [VMEM] * 7,
        [pltpu.VMEM((tok_rows, up_query.shape[0]), jnp.bfloat16)],
        2 * tok_rows * (up_query.size + up_key.size),
        2 * (up_query.size + up_key.size),
        limit=16,
    )(x_index, query_latent, query_first, query_second, up_query, up_key, query_cos, query_sin)

    key_parts = [key_at[:, part * TILE : (part + 1) * TILE] for part in range(2 * len(near))]

    query_at = own_positions.reshape(-1, 1)

    def stage(sources, places, state, last=False):
        return attend(
            queries,
            jnp.concatenate([key_parts[place] for place in places], axis=1),
            query_at,
            sources,
            state,
            up_value if last else None,
        )

    far = [send(part, other_core) for part in near[:3]]
    state = stage(near[:3], [0, 1, 2], ())
    near[3], state = lax.optimization_barrier((near[3], state))
    far.append(send(near[3], other_core))
    state = stage(far[:3], [4, 5, 6], state)
    return stage([near[3], far[3]], [3, 7], state, last=True)


def solution(mesh):
    placed = (
        P("ctx", "head"),
        P("head", None),
        P("head", None),
        P(),
        P(),
        P(None, "head"),
        P(None, "head"),
        P(None, "head"),
        P(),
    )
    return jax.shard_map(
        body, mesh=mesh, in_specs=placed, out_specs=P("ctx", "head"), check_vma=False
    )
```
